32 devices in a mesh: rep: 4 (over x, core), shard: 8 (over z, y).
Axes of the slice: x: 2, y: 2, z: 4, core: 2. Of those that a mesh axis runs over, the one named last changes fastest.
Arguments:
- weight: bfloat16 [4, 8, 512, 2048], P('rep', None, 'shard'), may hold values from -3 to 3
- tracker: float32 [4, 8, 512, 2048], P('rep', None, 'shard'), may hold values from -40 to 40, as said below
- grad_new: bfloat16 [4, 8, 512, 2048], P('rep', None, 'shard'), may hold values from -6 to 6
- grad_old: bfloat16 [4, 8, 512, 2048], P('rep', None, 'shard'), may hold values from -6 to 6
- mix_keep: int32 [4, 2], replicated, may hold values from 4 to 12, as said below
Outputs:
- new_weight: bfloat16 [4, 8, 512, 2048], P('rep', None, 'shard')
- new_tracker: float32 [4, 8, 512, 2048], P('rep', None, 'shard')
- update: bfloat16 [4, 8, 512, 2048], P('rep', None, 'shard')
The draws below stay inside these ranges and needn't reach their ends.
Inputs may be any that keep to these rules, and one draw needn't show every extreme that they name: `mix_keep`: every entry is one of the integers 4 to 12; some entry equals 4 and some equals 12. `tracker`: finite real values.
All inputs are finite; a program needn't handle non-finite values.
Results may differ from the reference program's by a relative error of at most 0.023.
Values may be sent and summed in bfloat16 or wider, within the bound.
No kernel may reach another device: no remote copies, remote signals or barrier semaphores. Data moves between devices by JAX's collectives and lax.ppermute only.
A program may use at most 128 MiB of HBM per device.

```python
import math
import jax
import jax.numpy as jnp
import numpy as np
from jax import lax

M = 512
N = 2048
NS_STEPS = 5
ROUNDS = 2
REPS = 4
EXPERTS = 8


def draw_tracker(key, part):
    key_noise, key_rows, key_cols = jax.random.split(key, 3)
    full_shape = (REPS, EXPERTS, M, N)
    log_low = math.log(0.3)
    log_high = math.log(3.0)
    base_noise = jnp.clip(jax.random.normal(key_noise, full_shape, jnp.float32), -4.0, 4.0)
    row_scale = jnp.exp(jax.random.uniform(key_rows, (REPS, EXPERTS, M, 1), jnp.float32, log_low, log_high))
    col_scale = jnp.exp(jax.random.uniform(key_cols, (REPS, EXPERTS, 1, N), jnp.float32, log_low, log_high))
    return base_noise * row_scale * col_scale


def draw_mix_keep(key, part):
    key_base, key_top, key_bottom = jax.random.split(key, 3)
    total_count = REPS * ROUNDS
    entries = jax.random.randint(key_base, (total_count,), 4, 13)
    top_pos = jax.random.randint(key_top, (), 0, total_count)
    bottom_pos = (top_pos + 1 + jax.random.randint(key_bottom, (), 0, total_count - 1)) % total_count
    entries = entries.at[top_pos].set(12).at[bottom_pos].set(4)
    return entries.reshape(REPS, ROUNDS).astype(jnp.int32)


def block_scale(stream_key, shape, shards, low, largest):
    def one(position, parts):
        draws = jax.random.uniform(jax.random.fold_in(jax.random.fold_in(stream_key, 6), position), (parts,), jnp.float32, low / len(shards), largest / len(shards))
        return jnp.repeat(jnp.exp(draws), shape[position] // parts).reshape((-1,) + (1,) * (len(shape) - position - 1))

    loudness = one(*shards[0])
    for cut in shards[1:]:
        loudness = loudness * one(*cut)
    return loudness


def scatter_about(stream_key, extent, width, bound, shards=(), held_as=jnp.bfloat16):
    array = jax.random.normal(stream_key, extent, jnp.float32) * width
    if len(shards) > 0:
        array = block_scale(stream_key, extent, shards, -0.22, 0.18) * array
    return jnp.clip(array, min=-bound, max=bound).astype(held_as)


def setup_inputs(seed: int = 0) -> dict:
    splits = jax.random.split(jax.random.key(seed), 6)
    return {
        "weight": scatter_about(splits[0], (REPS, EXPERTS, M, N), 0.5, 3.0, ((0, 4), (2, 8))),
        "tracker": draw_tracker(jax.random.fold_in(splits[5], 71), 0),
        "grad_new": scatter_about(splits[2], (REPS, EXPERTS, M, N), 1.0, 6.0, ((0, 4), (2, 8))),
        "grad_old": scatter_about(splits[3], (REPS, EXPERTS, M, N), 1.0, 6.0, ((0, 4), (2, 8))),
        "mix_keep": draw_mix_keep(jax.random.fold_in(splits[5], 71), 0),
    }


coeff_a = 3.4445
coeff_b = -4.775
coeff_c = 2.0315
learn_rate = 0.05

def orthogonalize(matrix):
    update_scale = 0.2 * math.sqrt(max(M, N))
    values = matrix.astype(jnp.float32)
    frob_norm = jnp.sqrt(jnp.sum(values * values))
    iterate = (values / (frob_norm + 1e-07)).astype(jnp.bfloat16)
    for iteration in range(NS_STEPS):
        gram_matrix = jnp.dot(iterate, iterate.T, preferred_element_type=jnp.float32).astype(jnp.bfloat16)
        square = jnp.dot(gram_matrix, gram_matrix, preferred_element_type=jnp.float32)
        polynomial = (coeff_b * gram_matrix.astype(jnp.float32) + coeff_c * square).astype(jnp.bfloat16)
        product = jnp.dot(polynomial, iterate, preferred_element_type=jnp.float32)
        iterate = (coeff_a * iterate.astype(jnp.float32) + product).astype(jnp.bfloat16)
    return (update_scale * iterate.astype(jnp.float32)).astype(jnp.bfloat16)

def reference(weight, tracker, grad_new, grad_old, mix_keep):
    replica_ids = np.arange(REPS)
    mixed_w = weight
    mixed_y = tracker
    for round_index in range(ROUNDS):
        partner_rows = replica_ids ^ 1 << round_index
        keep_column = mix_keep[:, round_index].astype(jnp.float32)
        own_share = (keep_column / 16.0)[:, None, None, None]
        other_share = ((16.0 - keep_column) / 16.0)[:, None, None, None]
        mixed_w = (own_share * mixed_w.astype(jnp.float32) + other_share * mixed_w[partner_rows].astype(jnp.float32)).astype(jnp.bfloat16)
        mixed_y = own_share * mixed_y + other_share * mixed_y[partner_rows]
    new_tracker = mixed_y + grad_new.astype(jnp.float32) - grad_old.astype(jnp.float32)
    rounded = lax.optimization_barrier(new_tracker.astype(jnp.bfloat16))
    matrices = rounded.reshape(REPS * EXPERTS, M, N)
    update = lax.map(orthogonalize, matrices).reshape(REPS, EXPERTS, M, N)
    new_weight = (mixed_w.astype(jnp.float32) - learn_rate * update.astype(jnp.float32)).astype(jnp.bfloat16)
    return (new_weight, new_tracker, update)
```

```python
import math

import jax
import jax.numpy as jnp
from jax import lax
from jax.experimental import pallas as pl
from jax.experimental.pallas import tpu as pltpu
from jax.sharding import PartitionSpec as P

NS_STEPS = 5
CHUNKS = 4

coeff_a = 3.4445
coeff_b = -4.775
coeff_c = 2.0315
learn_rate = 0.05

F32 = jnp.float32
BF16 = jnp.bfloat16
ANY = pl.BlockSpec(memory_space=pl.ANY)
SMEM = pl.BlockSpec(memory_space=pltpu.SMEM)
MIB = 1 << 20


def swapped(values, axis, bit):
    return lax.ppermute(values, axis, [(i, i ^ 1 << bit) for i in range(lax.axis_size(axis))])


def cost(flops, moved):
    return pl.CostEstimate(flops=int(flops), bytes_accessed=int(moved), transcendentals=0)


def params(mib):
    return pltpu.CompilerParams(vmem_limit_bytes=mib * MIB)


def slabs(experts):
    return experts // 4 if experts % 4 == 0 else 1


def mix_body(share, own, near, far, far_near, grad_new, grad_old, *rest):
    tracker_out, rounded_out = rest[-2:]
    mixed = (
        share[0] * own[...]
        + share[1] * near[...].astype(F32)
        + share[2] * far[...].astype(F32)
        + share[3] * far_near[...].astype(F32)
    )
    tracker = mixed + grad_new[...].astype(F32) - grad_old[...].astype(F32)
    tracker_out[...] = tracker
    rounded_out[...] = tracker.astype(BF16)


def mix_chunk(chunk, share, own, near, far, far_near, grad_new, grad_old, done):
    experts, rows, columns = own.shape
    width = far.shape[2]
    slab = slabs(experts)
    whole = pl.BlockSpec((slab, rows, width), lambda i: (i, 0, chunk))
    part = pl.BlockSpec((slab, rows, width), lambda i: (i, 0, 0))
    operands = [share, own, near, far, far_near, grad_new, grad_old]
    in_specs = [SMEM, whole, whole, part, part, whole, whole]
    aliases = {}
    if done is not None:
        aliases = {len(operands): 0}
        operands.append(done)
        in_specs.append(ANY)
    size = experts * rows * width
    return pl.pallas_call(
        mix_body,
        grid=(experts // slab,),
        in_specs=in_specs,
        out_specs=(whole, part),
        out_shape=(
            jax.ShapeDtypeStruct(own.shape, F32),
            jax.ShapeDtypeStruct(far.shape, BF16),
        ),
        input_output_aliases=aliases,
        compiler_params=params(24),
        cost_estimate=cost(12 * size, 20 * size),
        name="mix",
    )(*operands)


def split(values):
    high = values.astype(BF16)
    return high, (values - high.astype(F32)).astype(BF16)


def times(left, right):
    return jnp.dot(left, right, preferred_element_type=F32)


def diagonal(size):
    return lax.broadcasted_iota(jnp.int32, (size, size), 0) == lax.broadcasted_iota(
        jnp.int32, (size, size), 1
    )


def polynomial_body(scale, gram_ref, high_ref, low_ref, gram_held, poly_held):
    gram = gram_ref[0]
    size = gram.shape[0]
    on_diagonal = diagonal(size)
    square_norm = jnp.sum(
        jnp.sum(jnp.where(on_diagonal, gram, 0.0), axis=0, keepdims=True), axis=1, keepdims=True
    )
    inverse = 1.0 / (jnp.sqrt(square_norm) + 1e-07)
    gram_held[...] = gram * inverse * inverse
    poly_held[...] = jnp.where(on_diagonal, 1.0, 0.0)

    def step(last):
        gram = gram_held[...]
        gram_high, gram_low = split(gram)
        shift = (
            coeff_b * gram_high.astype(F32) + coeff_c * times(gram_high, gram_high)
        ).astype(BF16)
        poly = poly_held[...]
        poly_high, poly_low = split(poly)
        poly_held[...] = coeff_a * poly + times(shift, poly_high) + times(shift, poly_low)
        if not last:
            half = coeff_a * gram + times(shift, gram_high) + times(shift, gram_low)
            half_high, half_low = split(half)
            gram_held[...] = coeff_a * half + times(half_high, shift) + times(half_low, shift)

    @pl.loop(0, NS_STEPS - 1)
    def _(_):
        step(False)

    step(True)
    high, low = split(poly_held[...] * (scale * inverse))
    high_ref[0] = high
    low_ref[0] = low


def polynomial(gram, scale):
    count, size, _ = gram.shape
    block = pl.BlockSpec((1, size, size), lambda i: (i, 0, 0))
    kept = jax.ShapeDtypeStruct(gram.shape, BF16)

    def body(*refs):
        polynomial_body(scale, *refs)

    return pl.pallas_call(
        body,
        grid=(count,),
        in_specs=[block],
        out_specs=(block, block),
        out_shape=(kept, kept),
        scratch_shapes=[pltpu.VMEM((size, size), F32), pltpu.VMEM((size, size), F32)],
        compiler_params=params(32),
        cost_estimate=cost(2 * 29 * count * size**3, 8 * count * size**2),
        name="polynomial",
    )(gram)


def apply_body(high, low, values, out):
    out[0] = (times(high[0], values[0]) + times(low[0], values[0])).astype(BF16)


def apply_polynomial(high, low, values):
    count, size, width = values.shape
    square = pl.BlockSpec((1, size, size), lambda i: (i, 0, 0))
    block = pl.BlockSpec((1, size, width), lambda i: (i, 0, 0))
    return pl.pallas_call(
        apply_body,
        grid=(count,),
        in_specs=[square, square, block],
        out_specs=block,
        out_shape=jax.ShapeDtypeStruct(values.shape, BF16),
        compiler_params=params(24),
        cost_estimate=cost(4 * count * size**2 * width, 4 * count * size * (size + width)),
        name="apply",
    )(high, low, values)


def settle_body(share, own, far, update, *rest):
    weight_out, update_out = rest[-2:]
    mixed = (share[4] * own[...].astype(F32) + share[5] * far[...].astype(F32)).astype(BF16)
    taken = update[...]
    weight_out[...] = (mixed.astype(F32) - learn_rate * taken.astype(F32)).astype(BF16)
    update_out[...] = taken


def settle_chunk(chunk, share, own, far, update, done):
    experts, rows, columns = own.shape
    width = update.shape[2]
    slab = slabs(experts)
    whole = pl.BlockSpec((slab, rows, width), lambda i: (i, 0, chunk))
    part = pl.BlockSpec((slab, rows, width), lambda i: (i, 0, 0))
    operands = [share, own, far, update]
    in_specs = [SMEM, whole, whole, part]
    aliases = {}
    if done is not None:
        aliases = {len(operands): 0, len(operands) + 1: 1}
        operands += done
        in_specs += [ANY, ANY]
    size = experts * rows * width
    kept = jax.ShapeDtypeStruct(own.shape, BF16)
    return pl.pallas_call(
        settle_body,
        grid=(experts // slab,),
        in_specs=in_specs,
        out_specs=(whole, whole),
        out_shape=(kept, kept),
        input_output_aliases=aliases,
        compiler_params=params(24),
        cost_estimate=cost(8 * size, 10 * size),
        name="settle",
    )(*operands)


def exchange(values):
    return lax.all_to_all(values, "shard", split_axis=0, concat_axis=0, tiled=True)


def local(weight, tracker, grad_new, grad_old, mix_keep):
    shards = lax.axis_size("shard")
    _, experts, rows, columns = tracker.shape
    each = experts // shards
    size = shards * rows
    chunks = CHUNKS
    width = columns // chunks
    weight, tracker, grad_new, grad_old = (
        values.reshape(experts, rows, columns) for values in (weight, tracker, grad_new, grad_old)
    )

    rep_index = lax.axis_index("rep")
    keep = mix_keep.astype(F32) / 16.0
    first, second = keep[rep_index, 0], keep[rep_index, 1]
    far_first = keep[rep_index ^ 2, 0]
    share = jnp.stack(
        [
            second * first,
            second * (1.0 - first),
            (1.0 - second) * far_first,
            (1.0 - second) * (1.0 - far_first),
            second,
            1.0 - second,
        ]
    )

    far = []
    for chunk in range(chunks):
        sent = lax.slice_in_dim(tracker, chunk * width, (chunk + 1) * width, axis=2).astype(BF16)
        far.append(swapped(sent, "rep", 1))
    near = swapped(tracker.astype(BF16), "rep", 0)
    new_tracker = None
    held = []
    gram = None
    for chunk in range(chunks):
        far_near = swapped(far[chunk], "rep", 0)
        new_tracker, rounded = mix_chunk(
            chunk, share, tracker, near, far[chunk], far_near, grad_new, grad_old, new_tracker
        )
        matrix = exchange(rounded).reshape(shards, each, rows, width)
        matrix = matrix.swapaxes(0, 1).reshape(each, size, width)
        held.append(matrix)
        part = jnp.einsum("kmn,kpn->kmp", matrix, matrix, preferred_element_type=F32)
        gram = part if gram is None else gram + part

    weight_near = swapped(weight, "rep", 0)
    weight_own = (
        first * weight.astype(F32) + (1.0 - first) * weight_near.astype(F32)
    ).astype(BF16)
    weight_own, _ = lax.optimization_barrier((weight_own, far[-1]))
    weight_far = swapped(weight_own, "rep", 1)

    high, low = polynomial(gram, 0.2 * math.sqrt(max(size, columns)))
    done = None
    for chunk in range(chunks):
        update = apply_polynomial(high, low, held[chunk])
        update = update.reshape(each, shards, rows, width).swapaxes(0, 1)
        update = exchange(update.reshape(experts, rows, width))
        done = settle_chunk(chunk, share, weight_own, weight_far, update, done)
    shape = (1, experts, rows, columns)
    return done[0].reshape(shape), new_tracker.reshape(shape), done[1].reshape(shape)


def solution(mesh):
    spec = P("rep", None, "shard", None)
    return jax.shard_map(
        local,
        mesh=mesh,
        in_specs=(spec, spec, spec, spec, P()),
        out_specs=(spec, spec, spec),
        check_vma=False,
    )
```

```python
import math

import jax
import jax.numpy as jnp
from jax import lax
from jax.experimental import pallas as pl
from jax.experimental.pallas import tpu as pltpu
from jax.sharding import PartitionSpec as P

NS_STEPS = 5

coeff_a = 3.4445
coeff_b = -4.775
coeff_c = 2.0315
learn_rate = 0.05

F32 = jnp.float32
BF16 = jnp.bfloat16
MIB = 1 << 20


def swapped(values, axis, offset):
    return lax.ppermute(values, axis, [(i, i ^ offset) for i in range(lax.axis_size(axis))])


def cost(flops, moved):
    return pl.CostEstimate(flops=int(flops), bytes_accessed=int(moved), transcendentals=0)


def params(mib):
    return pltpu.CompilerParams(vmem_limit_bytes=mib * MIB)


def split(values):
    high = values.astype(BF16)
    return high, (values - high.astype(F32)).astype(BF16)


def times(left, right):
    return jnp.dot(left, right, preferred_element_type=F32)


def orthogonalize_body(scale, count, *refs):
    blocks, outs = refs[:count], refs[count : 2 * count]
    held, gram_held, poly_held = refs[2 * count :]
    rows = blocks[0].shape[1]
    for place, block in enumerate(blocks):
        held[pl.ds(place * rows, rows), :] = block[0]
    size = held.shape[0]
    gram = lax.dot_general(
        held[...], held[...], (((1,), (1,)), ((), ())), preferred_element_type=F32
    )
    on_diagonal = lax.broadcasted_iota(jnp.int32, (size, size), 0) == lax.broadcasted_iota(
        jnp.int32, (size, size), 1
    )
    square_norm = jnp.sum(
        jnp.sum(jnp.where(on_diagonal, gram, 0.0), axis=0, keepdims=True), axis=1, keepdims=True
    )
    inverse = 1.0 / (jnp.sqrt(square_norm) + 1e-07)
    gram_held[...] = gram * inverse * inverse
    poly_held[...] = jnp.where(on_diagonal, 1.0, 0.0)

    def step(last):
        gram = gram_held[...]
        gram_high, gram_low = split(gram)
        shift = (
            coeff_b * gram_high.astype(F32) + coeff_c * times(gram_high, gram_high)
        ).astype(BF16)
        poly = poly_held[...]
        poly_high, poly_low = split(poly)
        poly_held[...] = coeff_a * poly + times(shift, poly_high) + times(shift, poly_low)
        if not last:
            half = coeff_a * gram + times(shift, gram_high) + times(shift, gram_low)
            half_high, half_low = split(half)
            gram_held[...] = coeff_a * half + times(half_high, shift) + times(half_low, shift)

    @pl.loop(0, NS_STEPS - 1)
    def _(_):
        step(False)

    step(True)
    high, low = split(poly_held[...] * (scale * inverse))
    update = (times(high, held[...]) + times(low, held[...])).astype(BF16)
    for place, out in enumerate(outs):
        out[0] = update[place * rows : (place + 1) * rows]


def orthogonalize(blocks, scale):
    count = len(blocks)
    each, rows, columns = blocks[0].shape
    size = count * rows
    block = pl.BlockSpec((1, rows, columns), lambda i: (i, 0, 0))
    flops = 2 * each * size * size * (29 * size + 3 * columns)

    def body(*refs):
        orthogonalize_body(scale, count, *refs)

    return pl.pallas_call(
        body,
        grid=(each,),
        in_specs=[block] * count,
        out_specs=[block] * count,
        out_shape=[jax.ShapeDtypeStruct(blocks[0].shape, BF16)] * count,
        scratch_shapes=[
            pltpu.VMEM((size, columns), BF16),
            pltpu.VMEM((size, size), F32),
            pltpu.VMEM((size, size), F32),
        ],
        compiler_params=params(40),
        cost_estimate=cost(flops, 4 * each * size * columns),
        name="orthogonalize",
    )(*blocks)


def grouped(shards):
    groups = []
    top = shards
    for length in (shards // 8, shards // 8, shards // 4, shards // 2):
        if length:
            top -= length
            groups.append((top, length))
    return groups if top == 0 else [(0, shards)]


def local(weight, tracker, grad_new, grad_old, mix_keep):
    shards = lax.axis_size("shard")
    _, experts, rows, columns = tracker.shape
    each = experts // shards
    shape = (shards, each, rows, columns)
    weight, tracker, grad_new, grad_old = (
        values.reshape(shape) for values in (weight, tracker, grad_new, grad_old)
    )
    here = lax.axis_index("shard")
    rep_index = lax.axis_index("rep")
    keep = mix_keep.astype(F32) / 16.0
    first, second = keep[rep_index, 0], keep[rep_index, 1]

    def taken(values, start, length):
        return lax.dynamic_slice_in_dim(values, start, length, axis=0)

    new_tracker = jnp.zeros(shape, F32)
    blocks = [None] * shards
    far = None
    for lowest, length in grouped(shards):
        start = (here ^ lowest) // length * length
        own = taken(tracker, start, length)
        near = swapped(own.astype(BF16), "rep", 1)
        mixed = first * own + (1.0 - first) * near.astype(F32)
        far = swapped(mixed.astype(BF16), "rep", 2)
        group = second * mixed + (1.0 - second) * far.astype(F32)
        group += taken(grad_new, start, length).astype(F32)
        group -= taken(grad_old, start, length).astype(F32)
        for offset in reversed(range(lowest, lowest + length)):
            block = taken(group, (here ^ offset) % length, 1)[0].astype(BF16)
            blocks[offset] = swapped(block, "shard", offset) if offset else block
        new_tracker = lax.dynamic_update_slice_in_dim(new_tracker, group, start, axis=0)

    weight_near = swapped(weight, "rep", 1)
    weight_own = (
        first * weight.astype(F32) + (1.0 - first) * weight_near.astype(F32)
    ).astype(BF16)
    weight_own, _ = lax.optimization_barrier((weight_own, far))
    weight_far = swapped(weight_own, "rep", 2)
    mixed_weight = (
        second * weight_own.astype(F32) + (1.0 - second) * weight_far.astype(F32)
    ).astype(BF16)

    scale = 0.2 * math.sqrt(max(shards * rows, columns))
    updates = orthogonalize(blocks, scale)
    update = jnp.zeros(shape, BF16)
    new_weight = jnp.zeros(shape, BF16)
    for offset in reversed(range(shards)):
        block = updates[offset]
        block = swapped(block, "shard", offset) if offset else block
        place = here ^ offset
        kept = taken(mixed_weight, place, 1)[0]
        settled = (kept.astype(F32) - learn_rate * block.astype(F32)).astype(BF16)
        update = lax.dynamic_update_slice_in_dim(update, block[None], place, axis=0)
        new_weight = lax.dynamic_update_slice_in_dim(new_weight, settled[None], place, axis=0)
    shape = (1, experts, rows, columns)
    return new_weight.reshape(shape), new_tracker.reshape(shape), update.reshape(shape)


def solution(mesh):
    spec = P("rep", None, "shard", None)
    return jax.shard_map(
        local,
        mesh=mesh,
        in_specs=(spec, spec, spec, spec, P()),
        out_specs=(spec, spec, spec),
        check_vma=False,
    )
```

```python
import math

import jax
import jax.numpy as jnp
from jax import lax
from jax.experimental import pallas as pl
from jax.experimental.pallas import tpu as pltpu
from jax.sharding import PartitionSpec as P

NS_STEPS = 5

coeff_a = 3.4445
coeff_b = -4.775
coeff_c = 2.0315
learn_rate = 0.05

F32 = jnp.float32
BF16 = jnp.bfloat16
ANY = pl.BlockSpec(memory_space=pl.ANY)
MIB = 1 << 20


def swapped(values, axis, offset):
    return lax.ppermute(values, axis, [(i, i ^ offset) for i in range(lax.axis_size(axis))])


def cost(flops, moved):
    return pl.CostEstimate(flops=int(flops), bytes_accessed=int(moved), transcendentals=0)


def params(mib):
    return pltpu.CompilerParams(vmem_limit_bytes=mib * MIB)


def split(values):
    high = values.astype(BF16)
    return high, (values - high.astype(F32)).astype(BF16)


def times(left, right):
    return jnp.dot(left, right, preferred_element_type=F32)


def orthogonalize_body(scale, count, here, *refs):
    blocks, out = refs[:count], refs[count]
    held, made, gram_held, poly_held, in_sems, out_sems = refs[count + 1 :]
    rows = blocks[0].shape[1]
    size, columns = held.shape
    matrix = pl.program_id(0)
    copies = []
    for offset, block in enumerate(blocks):
        start = pl.multiple_of((here[0] ^ offset) * rows, rows)
        copies.append(
            pltpu.make_async_copy(
                block.at[matrix], held.at[pl.ds(start, rows), :], in_sems.at[offset]
            )
        )
    for copy in copies:
        copy.start()
    for copy in copies:
        copy.wait()

    gram = lax.dot_general(
        held[...], held[...], (((1,), (1,)), ((), ())), preferred_element_type=F32
    )
    on_diagonal = lax.broadcasted_iota(jnp.int32, (size, size), 0) == lax.broadcasted_iota(
        jnp.int32, (size, size), 1
    )
    square_norm = jnp.sum(
        jnp.sum(jnp.where(on_diagonal, gram, 0.0), axis=0, keepdims=True), axis=1, keepdims=True
    )
    inverse = 1.0 / (jnp.sqrt(square_norm) + 1e-07)
    gram_held[...] = gram * inverse * inverse

    def step(first, last):
        gram = gram_held[...]
        gram_high, gram_low = split(gram)
        shift = (
            coeff_b * gram_high.astype(F32) + coeff_c * times(gram_high, gram_high)
        ).astype(BF16)
        if first:
            poly_held[...] = jnp.where(on_diagonal, coeff_a, 0.0) + shift.astype(F32)
        else:
            poly = poly_held[...]
            poly_high, poly_low = split(poly)
            poly_held[...] = coeff_a * poly + times(shift, poly_high) + times(shift, poly_low)
        if not last:
            half = coeff_a * gram + times(shift, gram_high) + times(shift, gram_low)
            half_high, half_low = split(half)
            gram_held[...] = coeff_a * half + times(half_high, shift) + times(half_low, shift)

    step(True, False)

    @pl.loop(0, NS_STEPS - 2)
    def _(_):
        step(False, False)

    step(False, True)
    high, low = split(poly_held[...] * (scale * inverse))
    parts = out_sems.shape[0]
    width = columns // parts
    copies = []
    for part in range(parts):
        here_columns = pl.ds(part * width, width)
        values = held[:, here_columns]
        made[:, here_columns] = (times(high, values) + times(low, values)).astype(BF16)
        copies.append(
            pltpu.make_async_copy(
                made.at[:, here_columns], out.at[matrix, :, here_columns], out_sems.at[part]
            )
        )
        copies[-1].start()
    for copy in copies:
        copy.wait()


def orthogonalize(blocks, here, scale):
    count = len(blocks)
    each, rows, columns = blocks[0].shape
    size = count * rows
    parts = 4 if columns % 512 == 0 else 1
    flops = 2 * each * size * size * (29 * size + 3 * columns)

    def body(*refs):
        orthogonalize_body(scale, count, *refs)

    return pl.pallas_call(
        body,
        grid_spec=pltpu.PrefetchScalarGridSpec(
            num_scalar_prefetch=1,
            grid=(each,),
            in_specs=[ANY] * count,
            out_specs=ANY,
            scratch_shapes=[
                pltpu.VMEM((size, columns), BF16),
                pltpu.VMEM((size, columns), BF16),
                pltpu.VMEM((size, size), F32),
                pltpu.VMEM((size, size), F32),
                pltpu.SemaphoreType.DMA((count,)),
                pltpu.SemaphoreType.DMA((parts,)),
            ],
        ),
        out_shape=jax.ShapeDtypeStruct((each, size, columns), BF16),
        compiler_params=params(32),
        cost_estimate=cost(flops, 4 * each * size * columns),
        name="orthogonalize",
    )(here.reshape(1), *blocks)


def local(weight, tracker, grad_new, grad_old, mix_keep):
    shards = lax.axis_size("shard")
    _, experts, rows, columns = tracker.shape
    each = experts // shards
    shape = (shards, each, rows, columns)
    weight, tracker, grad_new, grad_old = (
        values.reshape(shape) for values in (weight, tracker, grad_new, grad_old)
    )
    here = lax.axis_index("shard")
    rep_index = lax.axis_index("rep")
    keep = mix_keep.astype(F32) / 16.0
    first, second = keep[rep_index, 0], keep[rep_index, 1]

    unit = shards // 8 if shards % 8 == 0 else 0
    if unit:
        groups = [(low * unit, count * unit) for low, count in ((7, 1), (6, 1), (2, 2), (4, 2), (0, 2))]
        lead = (6 * unit, 2 * unit)
    else:
        groups = [(0, shards)]
        lead = groups[0]

    def place(lowest, length):
        return (here ^ lowest) // length * length

    def taken(values, lowest, length, start=0):
        return lax.dynamic_slice_in_dim(values, place(lowest, length) - start, length, axis=0)

    def blend(own, near):
        return first * own + (1.0 - first) * near.astype(F32)

    own = taken(tracker, *lead)
    lead_mixed = blend(own, swapped(own.astype(BF16), "rep", 1))
    lead_sent = lead_mixed.astype(BF16)
    tracker, lead_sent = lax.optimization_barrier((tracker, lead_sent))
    near = swapped(tracker.astype(BF16), "rep", 1)

    new_tracker = jnp.zeros(shape, F32)
    blocks = [None] * shards
    arrived = []
    for turn, (lowest, length) in enumerate(groups):
        if lead[0] <= lowest < lead[0] + lead[1]:
            mixed = taken(lead_mixed, lowest, length, place(*lead))
            sent = taken(lead_sent, lowest, length, place(*lead))
        else:
            mixed = blend(taken(tracker, lowest, length), taken(near, lowest, length))
            waits = arrived[0] if turn == 2 else blocks[groups[turn - 3][0]]
            sent, _ = lax.optimization_barrier((mixed.astype(BF16), waits))
        far = swapped(sent, "rep", 2)
        arrived.append(far)
        part = second * mixed + (1.0 - second) * far.astype(F32)
        part += taken(grad_new, lowest, length).astype(F32)
        part -= taken(grad_old, lowest, length).astype(F32)
        for offset in reversed(range(lowest, lowest + length)):
            block = lax.dynamic_index_in_dim(part, (here ^ offset) % length, 0, False)
            block = block.astype(BF16)
            blocks[offset] = swapped(block, "shard", offset) if offset else block
        new_tracker = lax.dynamic_update_slice_in_dim(
            new_tracker, part, place(lowest, length), axis=0
        )

    weight, _ = lax.optimization_barrier((weight, arrived[len(groups) // 2]))
    weight_near = swapped(weight, "rep", 1)
    weight_own = blend(weight.astype(F32), weight_near).astype(BF16)
    weight_own, _ = lax.optimization_barrier((weight_own, arrived[-1]))
    weight_far = swapped(weight_own, "rep", 2)
    mixed_weight = (
        second * weight_own.astype(F32) + (1.0 - second) * weight_far.astype(F32)
    ).astype(BF16)

    scale = 0.2 * math.sqrt(max(shards * rows, columns))
    update = orthogonalize(blocks, here, scale)
    update = update.reshape(each, shards, rows, columns).swapaxes(0, 1)
    update = lax.all_to_all(update, "shard", split_axis=0, concat_axis=0, tiled=True)
    new_weight = (mixed_weight.astype(F32) - learn_rate * update.astype(F32)).astype(BF16)
    shape = (1, experts, rows, columns)
    return new_weight.reshape(shape), new_tracker.reshape(shape), update.reshape(shape)


def solution(mesh):
    spec = P("rep", None, "shard", None)
    return jax.shard_map(
        local,
        mesh=mesh,
        in_specs=(spec, spec, spec, spec, P()),
        out_specs=(spec, spec, spec),
        check_vma=False,
    )
```

```python
import math

import jax
import jax.numpy as jnp
from jax import lax
from jax.experimental import pallas as pl
from jax.experimental.pallas import tpu as pltpu
from jax.sharding import PartitionSpec as P

NS_STEPS = 5

coeff_a = 3.4445
coeff_b = -4.775
coeff_c = 2.0315
learn_rate = 0.05

F32 = jnp.float32
BF16 = jnp.bfloat16
ANY = pl.BlockSpec(memory_space=pl.ANY)
MIB = 1 << 20


def swapped(values, axis, offset):
    return lax.ppermute(values, axis, [(i, i ^ offset) for i in range(lax.axis_size(axis))])


def cost(flops, moved):
    return pl.CostEstimate(flops=int(flops), bytes_accessed=int(moved), transcendentals=0)


def params(mib):
    return pltpu.CompilerParams(vmem_limit_bytes=mib * MIB)


def split(values):
    high = values.astype(BF16)
    return high, (values - high.astype(F32)).astype(BF16)


def times(left, right):
    return jnp.dot(left, right, preferred_element_type=F32)


def orthogonalize_body(scale, count, here, *refs):
    blocks, out = refs[:count], refs[count]
    held, made, gram_held, poly_held, in_sems, out_sems = refs[count + 1 :]
    rows = blocks[0].shape[1]
    size, columns = held.shape
    matrix = pl.program_id(0)
    copies = []
    for offset, block in enumerate(blocks):
        start = pl.multiple_of((here[0] ^ offset) * rows, rows)
        copies.append(
            pltpu.make_async_copy(
                block.at[matrix], held.at[pl.ds(start, rows), :], in_sems.at[offset]
            )
        )
    for copy in copies:
        copy.start()
    for copy in copies:
        copy.wait()

    gram = lax.dot_general(
        held[...], held[...], (((1,), (1,)), ((), ())), preferred_element_type=F32
    )
    on_diagonal = lax.broadcasted_iota(jnp.int32, (size, size), 0) == lax.broadcasted_iota(
        jnp.int32, (size, size), 1
    )
    square_norm = jnp.sum(
        jnp.sum(jnp.where(on_diagonal, gram, 0.0), axis=0, keepdims=True), axis=1, keepdims=True
    )
    inverse = 1.0 / (jnp.sqrt(square_norm) + 1e-07)
    gram_held[...] = gram * inverse * inverse

    def step(first, last):
        gram = gram_held[...]
        gram_high, gram_low = split(gram)
        shift = (
            coeff_b * gram_high.astype(F32) + coeff_c * times(gram_high, gram_high)
        ).astype(BF16)
        if first:
            poly_held[...] = jnp.where(on_diagonal, coeff_a, 0.0) + shift.astype(F32)
        else:
            poly = poly_held[...]
            poly_high, poly_low = split(poly)
            poly_held[...] = coeff_a * poly + times(shift, poly_high) + times(shift, poly_low)
        if not last:
            half = coeff_a * gram + times(shift, gram_high) + times(shift, gram_low)
            half_high, half_low = split(half)
            gram_held[...] = coeff_a * half + times(half_high, shift) + times(half_low, shift)

    step(True, False)

    @pl.loop(0, NS_STEPS - 2)
    def _(_):
        step(False, False)

    step(False, True)
    high, low = split(poly_held[...] * (scale * inverse))
    parts = out_sems.shape[0]
    width = columns // parts
    copies = []
    for part in range(parts):
        here_columns = pl.ds(part * width, width)
        values = held[:, here_columns]
        made[:, here_columns] = (times(high, values) + times(low, values)).astype(BF16)
        copies.append(
            pltpu.make_async_copy(
                made.at[:, here_columns], out.at[matrix, :, here_columns], out_sems.at[part]
            )
        )
        copies[-1].start()
    for copy in copies:
        copy.wait()


def orthogonalize(blocks, here, scale):
    count = len(blocks)
    each, rows, columns = blocks[0].shape
    size = count * rows
    parts = 4 if columns % 512 == 0 else 1
    flops = 2 * each * size * size * (29 * size + 3 * columns)

    def body(*refs):
        orthogonalize_body(scale, count, *refs)

    return pl.pallas_call(
        body,
        grid_spec=pltpu.PrefetchScalarGridSpec(
            num_scalar_prefetch=1,
            grid=(each,),
            in_specs=[ANY] * count,
            out_specs=ANY,
            scratch_shapes=[
                pltpu.VMEM((size, columns), BF16),
                pltpu.VMEM((size, columns), BF16),
                pltpu.VMEM((size, size), F32),
                pltpu.VMEM((size, size), F32),
                pltpu.SemaphoreType.DMA((count,)),
                pltpu.SemaphoreType.DMA((parts,)),
            ],
        ),
        out_shape=jax.ShapeDtypeStruct((each, size, columns), BF16),
        compiler_params=params(32),
        cost_estimate=cost(flops, 4 * each * size * columns),
        name="orthogonalize",
    )(here.reshape(1), *blocks)


def local(weight, tracker, grad_new, grad_old, mix_keep):
    shards = lax.axis_size("shard")
    _, experts, rows, columns = tracker.shape
    each = experts // shards
    shape = (shards, each, rows, columns)
    weight, tracker, grad_new, grad_old = (
        values.reshape(shape) for values in (weight, tracker, grad_new, grad_old)
    )
    here = lax.axis_index("shard")
    rep_index = lax.axis_index("rep")
    keep = mix_keep.astype(F32) / 16.0
    first, second = keep[rep_index, 0], keep[rep_index, 1]
    far_first = keep[rep_index ^ 2, 0]

    count = 8 if shards % 8 == 0 else 1
    length = shards // count
    paired = 2 if count > 1 else 1

    def place(group):
        return (here ^ (group * length)) // length * length

    def taken(values, group):
        return lax.dynamic_slice_in_dim(values, place(group), length, axis=0)

    def blend(share, own, near):
        return share * own + (1.0 - share) * near.astype(F32)

    def after(values, *others):
        return lax.optimization_barrier((values, others))[0]

    new_tracker = jnp.zeros(shape, F32)
    blocks = [None] * shards
    arrived = []
    for turn, group in enumerate(reversed(range(count))):
        if turn % paired == 0:
            size = paired * length
            base = place(group) // size * size
            source = after(tracker, arrived[0]) if turn >= 4 else tracker
            pair = lax.dynamic_slice_in_dim(source, base, size, axis=0)
            pair_near = swapped(pair.astype(BF16), "rep", 1)
        own = lax.dynamic_slice_in_dim(pair, place(group) - base, length, axis=0)
        near = lax.dynamic_slice_in_dim(pair_near, place(group) - base, length, axis=0)
        mixed = blend(first, own, near)
        if turn < 2:
            far = swapped(own.astype(BF16), "rep", 2)
            far_mixed = blend(far_first, far.astype(F32), swapped(far, "rep", 1))
        else:
            sent = after(mixed.astype(BF16), arrived[turn - 2])
            if turn in (3, 5, 7):
                sent = after(sent, blocks[(8 - (turn - 1) // 2) * length])
            far = swapped(sent, "rep", 2)
            if turn == count - 1:
                far = after(far, blocks[4 * length], blocks[3 * length])
            far_mixed = far.astype(F32)
        arrived.append(far)
        part = second * mixed + (1.0 - second) * far_mixed
        part += taken(grad_new, group).astype(F32)
        part -= taken(grad_old, group).astype(F32)
        for offset in reversed(range(group * length, (group + 1) * length)):
            block = lax.dynamic_index_in_dim(part, (here ^ offset) % length, 0, False)
            block = block.astype(BF16)
            blocks[offset] = swapped(block, "shard", offset) if offset else block
        new_tracker = lax.dynamic_update_slice_in_dim(new_tracker, part, place(group), axis=0)

    weight = after(weight, arrived[count // 2])
    weight_near = swapped(weight, "rep", 1)
    weight_own = blend(first, weight.astype(F32), weight_near).astype(BF16)
    weight_own = after(weight_own, arrived[-1])
    halves = jnp.split(weight_own, 2) if shards % 2 == 0 else [weight_own]
    halves_far = [swapped(half, "rep", 2) for half in halves]

    scale = 0.2 * math.sqrt(max(shards * rows, columns))
    update = orthogonalize(blocks, here, scale)
    update = after(update, halves_far[0])
    update = update.reshape(each, shards, rows, columns).swapaxes(0, 1)
    update = lax.all_to_all(update, "shard", split_axis=0, concat_axis=0, tiled=True)
    mixed_weight = jnp.concatenate(
        [
            blend(second, half.astype(F32), half_far).astype(BF16)
            for half, half_far in zip(halves, halves_far)
        ]
    )
    mixed_weight = lax.optimization_barrier(mixed_weight)
    new_weight = (mixed_weight.astype(F32) - learn_rate * update.astype(F32)).astype(BF16)
    shape = (1, experts, rows, columns)
    return new_weight.reshape(shape), new_tracker.reshape(shape), update.reshape(shape)


def solution(mesh):
    spec = P("rep", None, "shard", None)
    return jax.shard_map(
        local,
        mesh=mesh,
        in_specs=(spec, spec, spec, spec, P()),
        out_specs=(spec, spec, spec),
        check_vma=False,
    )
```

```python
import math

import jax
import jax.numpy as jnp
from jax import lax
from jax.experimental import pallas as pl
from jax.experimental.pallas import tpu as pltpu
from jax.sharding import PartitionSpec as P

NS_STEPS = 5

coeff_a = 3.4445
coeff_b = -4.775
coeff_c = 2.0315
learn_rate = 0.05

F32 = jnp.float32
BF16 = jnp.bfloat16
ANY = pl.BlockSpec(memory_space=pl.ANY)
MIB = 1 << 20


def swapped(values, axis, offset):
    return lax.ppermute(values, axis, [(i, i ^ offset) for i in range(lax.axis_size(axis))])


def cost(flops, moved):
    return pl.CostEstimate(flops=int(flops), bytes_accessed=int(moved), transcendentals=0)


def params(mib):
    return pltpu.CompilerParams(vmem_limit_bytes=mib * MIB)


def split(values):
    high = values.astype(BF16)
    return high, (values - high.astype(F32)).astype(BF16)


def times(left, right):
    return jnp.dot(left, right, preferred_element_type=F32)


def orthogonalize_body(scale, count, here, *refs):
    blocks, out = refs[:count], refs[count]
    held, made, gram_held, poly_held, in_sems, out_sems = refs[count + 1 :]
    rows = blocks[0].shape[1]
    size, columns = held.shape
    matrix = pl.program_id(0)
    copies = []
    for offset, block in enumerate(blocks):
        start = pl.multiple_of((here[0] ^ offset) * rows, rows)
        copies.append(
            pltpu.make_async_copy(
                block.at[matrix], held.at[pl.ds(start, rows), :], in_sems.at[offset]
            )
        )
    for copy in copies:
        copy.start()
    for copy in copies:
        copy.wait()

    gram = lax.dot_general(
        held[...], held[...], (((1,), (1,)), ((), ())), preferred_element_type=F32
    )
    on_diagonal = lax.broadcasted_iota(jnp.int32, (size, size), 0) == lax.broadcasted_iota(
        jnp.int32, (size, size), 1
    )
    square_norm = jnp.sum(
        jnp.sum(jnp.where(on_diagonal, gram, 0.0), axis=0, keepdims=True), axis=1, keepdims=True
    )
    inverse = 1.0 / (jnp.sqrt(square_norm) + 1e-07)
    gram_held[...] = gram * inverse * inverse

    def step(first, last):
        gram = gram_held[...]
        gram_high, gram_low = split(gram)
        shift = (
            coeff_b * gram_high.astype(F32) + coeff_c * times(gram_high, gram_high)
        ).astype(BF16)
        if first:
            poly_held[...] = jnp.where(on_diagonal, coeff_a, 0.0) + shift.astype(F32)
        else:
            poly = poly_held[...]
            poly_high, poly_low = split(poly)
            poly_held[...] = coeff_a * poly + times(shift, poly_high) + times(shift, poly_low)
        if not last:
            half = coeff_a * gram + times(shift, gram_high) + times(shift, gram_low)
            half_high, half_low = split(half)
            gram_held[...] = coeff_a * half + times(half_high, shift) + times(half_low, shift)

    step(True, False)

    @pl.loop(0, NS_STEPS - 2)
    def _(_):
        step(False, False)

    step(False, True)
    high, low = split(poly_held[...] * (scale * inverse))
    parts = out_sems.shape[0]
    width = columns // parts
    copies = []
    for part in range(parts):
        here_columns = pl.ds(part * width, width)
        values = held[:, here_columns]
        made[:, here_columns] = (times(high, values) + times(low, values)).astype(BF16)
        copies.append(
            pltpu.make_async_copy(
                made.at[:, here_columns], out.at[matrix, :, here_columns], out_sems.at[part]
            )
        )
        copies[-1].start()
    for copy in copies:
        copy.wait()


def orthogonalize(blocks, here, scale):
    count = len(blocks)
    each, rows, columns = blocks[0].shape
    size = count * rows
    parts = 4 if columns % 512 == 0 else 1
    flops = 2 * each * size * size * (29 * size + 3 * columns)

    def body(*refs):
        orthogonalize_body(scale, count, *refs)

    return pl.pallas_call(
        body,
        grid_spec=pltpu.PrefetchScalarGridSpec(
            num_scalar_prefetch=1,
            grid=(each,),
            in_specs=[ANY] * count,
            out_specs=ANY,
            scratch_shapes=[
                pltpu.VMEM((size, columns), BF16),
                pltpu.VMEM((size, columns), BF16),
                pltpu.VMEM((size, size), F32),
                pltpu.VMEM((size, size), F32),
                pltpu.SemaphoreType.DMA((count,)),
                pltpu.SemaphoreType.DMA((parts,)),
            ],
        ),
        out_shape=jax.ShapeDtypeStruct((each, size, columns), BF16),
        compiler_params=params(32),
        cost_estimate=cost(flops, 4 * each * size * columns),
        name="orthogonalize",
    )(here.reshape(1), *blocks)


def block_of(array, index):
    tail = array.shape[1:]
    return pl.BlockSpec((1,) + tail, lambda *args: (index(*args),) + (0,) * len(tail))


def in_hbm(array):
    return pltpu.with_memory_space_constraint(array, pltpu.HBM)


def run(body, name, steps, picks, operands, outs):
    return pl.pallas_call(
        body,
        grid_spec=pltpu.PrefetchScalarGridSpec(
            num_scalar_prefetch=1,
            grid=(steps,),
            in_specs=[
                pl.BlockSpec(memory_space=pltpu.SMEM) if index is None else block_of(array, index)
                for array, index in operands
            ],
            out_specs=[block_of(shape, index) for shape, index in outs],
        ),
        out_shape=[shape for shape, _ in outs],
        compiler_params=params(24),
        cost_estimate=cost(
            sum(array.size for array, _ in operands),
            sum(array.size * array.dtype.itemsize for array, _ in operands + outs),
        ),
        name=name,
    )(picks, *(array for array, _ in operands))


def by_step(step, picks):
    return step


def by_pick(step, picks):
    return picks[step]


def within(start, length):
    return lambda step, picks: jnp.clip(step - start, 0, length - 1)


def like(array, dtype, leading):
    return jax.ShapeDtypeStruct((leading,) + array.shape[1:], dtype)


def gather_body(picks, own, out):
    out[...] = own[...].astype(BF16)


def gather(picks, tracker):
    steps = picks.shape[0]
    return run(
        gather_body, "gather", steps, picks,
        [(in_hbm(tracker), by_pick)], [(like(tracker, BF16, steps), by_step)],
    )[0]


def base_body(picks, share, own, near, grad_new, grad_old, base, *sends):
    mixed = share[0] * own[...] + share[1] * near[...].astype(F32)
    base[...] = share[3] * mixed + (grad_new[...].astype(F32) - grad_old[...].astype(F32))
    sent = mixed.astype(BF16)
    for turn, send in enumerate(sends):
        @pl.when(pl.program_id(0) // 2 == turn)
        def _():
            send[...] = sent


def make_base(picks, share, tracker, near, grad_new, grad_old):
    steps = picks.shape[0]
    base, *sends = run(
        base_body, "base", steps, picks,
        [(share, None), (in_hbm(tracker), by_pick), (near, by_step)]
        + [(in_hbm(grad_new), by_pick), (in_hbm(grad_old), by_pick)],
        [(like(tracker, F32, steps), by_step)]
        + [(like(tracker, BF16, 2), within(start, 2)) for start in range(0, steps, 2)],
    )
    return base, sends


def place_body(count, picks, share, *refs):
    *leads, base = refs[: count + 1]
    fars, out = refs[count + 1 : -1], refs[-1]
    step = pl.program_id(0)
    for turn, lead in enumerate(leads):
        @pl.when(step == turn)
        def _():
            out[...] = lead[...]
    for turn, far in enumerate(fars):
        @pl.when((step >= count) & ((step - count) // 2 == turn))
        def _():
            out[...] = base[...] + share[4] * far[...].astype(F32)


def place_tracker(picks, share, leads, base, fars):
    steps, count = picks.shape[0], len(leads)
    return run(
        lambda *refs: place_body(count, *refs), "place", steps, picks,
        [(share, None)]
        + [(lead, within(turn, 1)) for turn, lead in enumerate(leads)]
        + [(base, within(count, steps - count))]
        + [(far, within(count + 2 * turn, 2)) for turn, far in enumerate(fars)],
        [(like(base, F32, steps), by_pick)],
    )[0]


def first_weight_body(picks, share, own, near, *outs):
    mixed = share[0] * own[...].astype(F32) + share[1] * near[...].astype(F32)
    for turn, out in enumerate(outs):
        @pl.when(pl.program_id(0) // 4 == turn)
        def _():
            out[...] = mixed.astype(BF16)


def first_weight(picks, share, weight, near):
    return run(
        first_weight_body, "first_weight", 8, picks,
        [(share, None), (in_hbm(weight), by_step), (near, by_step)],
        [(like(weight, BF16, 4), within(start, 4)) for start in (0, 4)],
    )


def second_weight_body(picks, share, *refs):
    out = refs[-1]
    for turn in range(2):
        @pl.when(pl.program_id(0) // 4 == turn)
        def _():
            own, far = refs[turn][...].astype(F32), refs[2 + turn][...].astype(F32)
            out[...] = (share[3] * own + share[4] * far).astype(BF16)


def second_weight(picks, share, owns, fars):
    halves = [(half, within(4 * turn, 4)) for turn, half in enumerate(owns)]
    halves += [(half, within(4 * turn, 4)) for turn, half in enumerate(fars)]
    return run(
        second_weight_body, "second_weight", 8, picks,
        [(share, None)] + halves, [(like(owns[0], BF16, 8), by_step)],
    )[0]


def settle_body(picks, mixed, update, weight_out, update_out):
    taken = update[...]
    weight_out[...] = (mixed[...].astype(F32) - learn_rate * taken.astype(F32)).astype(BF16)
    update_out[...] = taken


def settle(picks, mixed, update):
    kept = like(mixed, BF16, 8)
    return run(
        settle_body, "settle", 8, picks,
        [(mixed, by_step), (update, by_step)], [(kept, by_step), (kept, by_step)],
    )


def after(values, *others):
    return lax.optimization_barrier((values, others))[0]


def local(weight, tracker, grad_new, grad_old, mix_keep):
    shards = lax.axis_size("shard")
    _, experts, rows, columns = tracker.shape
    each = experts // shards
    length = shards // 8
    shape = (8, length, each, rows, columns)
    weight, tracker, grad_new, grad_old = (
        values.reshape(shape) for values in (weight, tracker, grad_new, grad_old)
    )
    here = lax.axis_index("shard")
    rep_index = lax.axis_index("rep")
    keep = mix_keep.astype(F32) / 16.0
    first, second = keep[rep_index, 0], keep[rep_index, 1]
    far_first = keep[rep_index ^ 2, 0]
    share = jnp.stack([first, 1.0 - first, far_first, second, 1.0 - second])

    order = (7, 6, 5, 4, 3, 2, 1, 0)
    picks = jnp.array(order, jnp.int32) ^ (here // length)

    def taken(values, turn):
        return lax.dynamic_slice_in_dim(values, picks[turn], 1, axis=0)

    blocks = [None] * shards
    ready = []

    def spread(part, group):
        part = part.astype(BF16).reshape(shape[1:])
        ready.append(part)
        for offset in reversed(range(group * length, (group + 1) * length)):
            block = part[0]
            if length > 1:
                block = lax.dynamic_index_in_dim(part, (here ^ offset) % length, 0, False)
            blocks[offset] = swapped(block, "shard", offset) if offset else block

    leads = [taken(tracker, turn).astype(BF16) for turn in range(2)]
    lead_fars = [swapped(lead, "rep", 2) for lead in leads]
    lead_nears = [swapped(lead, "rep", 1) for lead in leads]
    near = swapped(gather(picks[2:], after(tracker, leads)), "rep", 1)
    base, sends = make_base(picks[2:], share, tracker, near, grad_new, grad_old)

    lead_parts = []
    for turn in range(2):
        far = lead_fars[turn]
        mixed = first * taken(tracker, turn) + (1.0 - first) * lead_nears[turn].astype(F32)
        far_mixed = far_first * far.astype(F32)
        far_mixed += (1.0 - far_first) * swapped(far, "rep", 1).astype(F32)
        part = second * mixed + (1.0 - second) * far_mixed
        part += taken(grad_new, turn).astype(F32) - taken(grad_old, turn).astype(F32)
        lead_parts.append(part)
        spread(part, order[turn])

    halves = None
    arrived = list(lead_fars)
    fars = []
    for turn, sent in enumerate(sends):
        sent = after(sent, arrived[turn])
        if turn > 0:
            sent = after(sent, blocks[order[turn - 1] * length], ready[-1])
        far = swapped(sent, "rep", 2)
        arrived.append(far)
        if turn == 1:
            weight_near = swapped(after(weight, arrived[1]), "rep", 1)
            halves = first_weight(picks, share, weight, weight_near)
        if turn == 2:
            far = after(far, blocks[order[2] * length], halves[0])
        if turn > 0:
            far = after(far, ready[-1])
        fars.append(far)
        for step in range(2):
            part = base[2 * turn + step] + (1.0 - second) * far[step].astype(F32)
            spread(part, order[2 + 2 * turn + step])

    halves = [after(half, arrived[-1]) for half in halves]
    halves_far = [swapped(half, "rep", 2) for half in halves]

    scale = 0.2 * math.sqrt(max(shards * rows, columns))
    update = orthogonalize(blocks, here, scale)
    update = after(update, halves_far[0])
    update = update.reshape(each, shards, rows, columns).swapaxes(0, 1)
    update = lax.all_to_all(update, "shard", split_axis=0, concat_axis=0, tiled=True)
    new_tracker = place_tracker(picks, share, lead_parts, base, fars)
    mixed_weight = second_weight(picks, share, halves, halves_far)
    new_weight, update = settle(picks, mixed_weight, update.reshape(shape))
    shape = (1, experts, rows, columns)
    return new_weight.reshape(shape), new_tracker.reshape(shape), update.reshape(shape)


def solution(mesh):
    spec = P("rep", None, "shard", None)
    return jax.shard_map(
        local,
        mesh=mesh,
        in_specs=(spec, spec, spec, spec, P()),
        out_specs=(spec, spec, spec),
        check_vma=False,
    )
```

```python
import math

import jax
import jax.numpy as jnp
from jax import lax
from jax.experimental import pallas as pl
from jax.experimental.pallas import tpu as pltpu
from jax.sharding import PartitionSpec as P

NS_STEPS = 5

coeff_a = 3.4445
coeff_b = -4.775
coeff_c = 2.0315
learn_rate = 0.05

F32 = jnp.float32
BF16 = jnp.bfloat16
MIB = 1 << 20


def swapped(values, axis, offset):
    return lax.ppermute(values, axis, [(i, i ^ offset) for i in range(lax.axis_size(axis))])


def cost(flops, moved):
    return pl.CostEstimate(flops=int(flops), bytes_accessed=int(moved), transcendentals=0)


def params(mib):
    return pltpu.CompilerParams(vmem_limit_bytes=mib * MIB)


def split(values):
    high = values.astype(BF16)
    return high, (values - high.astype(F32)).astype(BF16)


def times(left, right):
    return jnp.dot(left, right, preferred_element_type=F32)


def orthogonalize_body(scale, count, *refs):
    blocks, outs = refs[:count], refs[count : 2 * count]
    held, gram_held, poly_held = refs[2 * count :]
    rows = blocks[0].shape[1]
    for place, block in enumerate(blocks):
        held[pl.ds(place * rows, rows), :] = block[0]
    size = held.shape[0]
    gram = lax.dot_general(
        held[...], held[...], (((1,), (1,)), ((), ())), preferred_element_type=F32
    )
    on_diagonal = lax.broadcasted_iota(jnp.int32, (size, size), 0) == lax.broadcasted_iota(
        jnp.int32, (size, size), 1
    )
    square_norm = jnp.sum(
        jnp.sum(jnp.where(on_diagonal, gram, 0.0), axis=0, keepdims=True), axis=1, keepdims=True
    )
    inverse = 1.0 / (jnp.sqrt(square_norm) + 1e-07)
    gram_held[...] = gram * inverse * inverse

    def step(first, last):
        gram = gram_held[...]
        gram_high, gram_low = split(gram)
        shift = (
            coeff_b * gram_high.astype(F32) + coeff_c * times(gram_high, gram_high)
        ).astype(BF16)
        if first:
            poly_held[...] = jnp.where(on_diagonal, coeff_a, 0.0) + shift.astype(F32)
        else:
            poly = poly_held[...]
            poly_high, poly_low = split(poly)
            poly_held[...] = coeff_a * poly + times(shift, poly_high) + times(shift, poly_low)
        if not last:
            half = coeff_a * gram + times(shift, gram_high) + times(shift, gram_low)
            half_high, half_low = split(half)
            gram_held[...] = coeff_a * half + times(half_high, shift) + times(half_low, shift)

    step(True, False)

    @pl.loop(0, NS_STEPS - 2)
    def _(_):
        step(False, False)

    step(False, True)
    high, low = split(poly_held[...] * (scale * inverse))
    update = (times(high, held[...]) + times(low, held[...])).astype(BF16)
    for place, out in enumerate(outs):
        out[0] = update[place * rows : (place + 1) * rows]


def orthogonalize(blocks, scale):
    count = len(blocks)
    each, rows, columns = blocks[0].shape
    size = count * rows
    block = pl.BlockSpec((1, rows, columns), lambda i: (i, 0, 0))
    flops = 2 * each * size * size * (29 * size + 3 * columns)

    def body(*refs):
        orthogonalize_body(scale, count, *refs)

    return pl.pallas_call(
        body,
        grid=(each,),
        in_specs=[block] * count,
        out_specs=[block] * count,
        out_shape=[jax.ShapeDtypeStruct(blocks[0].shape, BF16)] * count,
        scratch_shapes=[
            pltpu.VMEM((size, columns), BF16),
            pltpu.VMEM((size, size), F32),
            pltpu.VMEM((size, size), F32),
        ],
        compiler_params=params(40),
        cost_estimate=cost(flops, 4 * each * size * columns),
        name="orthogonalize",
    )(*blocks)


def grouped(shards):
    groups = []
    top = shards
    for length in (shards // 8, shards // 8, shards // 4, shards // 2):
        if length:
            top -= length
            groups.append((top, length))
    return groups if top == 0 else [(0, shards)]


def after(values, *others):
    return lax.optimization_barrier((values, others))[0]


def local(weight, tracker, grad_new, grad_old, mix_keep):
    shards = lax.axis_size("shard")
    _, experts, rows, columns = tracker.shape
    each = experts // shards
    shape = (shards, each, rows, columns)
    weight, tracker, grad_new, grad_old = (
        values.reshape(shape) for values in (weight, tracker, grad_new, grad_old)
    )
    here = lax.axis_index("shard")
    rep_index = lax.axis_index("rep")
    keep = mix_keep.astype(F32) / 16.0
    first, second = keep[rep_index, 0], keep[rep_index, 1]

    def taken(values, start, length):
        return lax.dynamic_slice_in_dim(values, start, length, axis=0)

    new_tracker = jnp.zeros(shape, F32)
    blocks = [None] * shards
    for turn, (lowest, length) in enumerate(grouped(shards)):
        if turn == 2:
            tracker = after(tracker, sent)
        start = (here ^ lowest) // length * length
        own = taken(tracker, start, length)
        near = swapped(own.astype(BF16), "rep", 1)
        mixed = first * own + (1.0 - first) * near.astype(F32)
        sent = mixed.astype(BF16)
        far = swapped(sent, "rep", 2)
        group = second * mixed + (1.0 - second) * far.astype(F32)
        group += taken(grad_new, start, length).astype(F32)
        group -= taken(grad_old, start, length).astype(F32)
        for offset in reversed(range(lowest, lowest + length)):
            block = taken(group, (here ^ offset) % length, 1)[0].astype(BF16)
            blocks[offset] = swapped(block, "shard", offset) if offset else block
        new_tracker = lax.dynamic_update_slice_in_dim(new_tracker, group, start, axis=0)

    weight_near = swapped(weight, "rep", 1)
    weight_own = (
        first * weight.astype(F32) + (1.0 - first) * weight_near.astype(F32)
    ).astype(BF16)
    weight_own = after(weight_own, far, blocks[1])
    weight_far = swapped(weight_own, "rep", 2)
    mixed_weight = (
        second * weight_own.astype(F32) + (1.0 - second) * weight_far.astype(F32)
    ).astype(BF16)

    scale = 0.2 * math.sqrt(max(shards * rows, columns))
    updates = orthogonalize(blocks, scale)
    update = jnp.zeros(shape, BF16)
    new_weight = jnp.zeros(shape, BF16)
    half = shards // 2
    order = list(range(1, half)) + list(reversed(range(half, shards))) + [0]
    received = [
        swapped(block, "shard", offset) if offset else block for offset, block in enumerate(updates)
    ]
    mixed_weight = after(mixed_weight, received[-1])
    for offset in order:
        block = received[offset]
        place = here ^ offset
        kept = taken(mixed_weight, place, 1)[0]
        settled = (kept.astype(F32) - learn_rate * block.astype(F32)).astype(BF16)
        update = lax.dynamic_update_slice_in_dim(update, block[None], place, axis=0)
        new_weight = lax.dynamic_update_slice_in_dim(new_weight, settled[None], place, axis=0)
    shape = (1, experts, rows, columns)
    return new_weight.reshape(shape), new_tracker.reshape(shape), update.reshape(shape)


def solution(mesh):
    spec = P("rep", None, "shard", None)
    return jax.shard_map(
        local,
        mesh=mesh,
        in_specs=(spec, spec, spec, spec, P()),
        out_specs=(spec, spec, spec),
        check_vma=False,
    )
```

```python
import math

import jax
import jax.numpy as jnp
from jax import lax
from jax.experimental import pallas as pl
from jax.experimental.pallas import tpu as pltpu
from jax.sharding import PartitionSpec as P

NS_STEPS = 5

coeff_a = 3.4445
coeff_b = -4.775
coeff_c = 2.0315
learn_rate = 0.05

F32 = jnp.float32
BF16 = jnp.bfloat16
MIB = 1 << 20


def swapped(values, axis, offset):
    return lax.ppermute(values, axis, [(i, i ^ offset) for i in range(lax.axis_size(axis))])


def cost(flops, moved):
    return pl.CostEstimate(flops=int(flops), bytes_accessed=int(moved), transcendentals=0)


def params(mib):
    return pltpu.CompilerParams(vmem_limit_bytes=mib * MIB)


def split(values):
    high = values.astype(BF16)
    return high, (values - high.astype(F32)).astype(BF16)


def times(left, right):
    return jnp.dot(left, right, preferred_element_type=F32)


def orthogonalize_body(scale, count, *refs):
    blocks, outs = refs[:count], refs[count : 2 * count]
    held, gram_held, poly_held = refs[2 * count :]
    rows = blocks[0].shape[1]
    for place, block in enumerate(blocks):
        held[pl.ds(place * rows, rows), :] = block[0]
    size = held.shape[0]
    gram = lax.dot_general(
        held[...], held[...], (((1,), (1,)), ((), ())), preferred_element_type=F32
    )
    on_diagonal = lax.broadcasted_iota(jnp.int32, (size, size), 0) == lax.broadcasted_iota(
        jnp.int32, (size, size), 1
    )
    square_norm = jnp.sum(
        jnp.sum(jnp.where(on_diagonal, gram, 0.0), axis=0, keepdims=True), axis=1, keepdims=True
    )
    inverse = 1.0 / (jnp.sqrt(square_norm) + 1e-07)
    gram_held[...] = gram * inverse * inverse

    def step(first, last):
        gram = gram_held[...]
        gram_high, gram_low = split(gram)
        shift = (
            coeff_b * gram_high.astype(F32) + coeff_c * times(gram_high, gram_high)
        ).astype(BF16)
        if first:
            poly_held[...] = jnp.where(on_diagonal, coeff_a, 0.0) + shift.astype(F32)
        else:
            poly = poly_held[...]
            poly_high, poly_low = split(poly)
            poly_held[...] = coeff_a * poly + times(shift, poly_high) + times(shift, poly_low)
        if not last:
            half = coeff_a * gram + times(shift, gram_high) + times(shift, gram_low)
            half_high, half_low = split(half)
            gram_held[...] = coeff_a * half + times(half_high, shift) + times(half_low, shift)

    step(True, False)

    @pl.loop(0, NS_STEPS - 2)
    def _(_):
        step(False, False)

    step(False, True)
    high, low = split(poly_held[...] * (scale * inverse))
    update = (times(high, held[...]) + times(low, held[...])).astype(BF16)
    for place, out in enumerate(outs):
        out[0] = update[place * rows : (place + 1) * rows]


def orthogonalize(blocks, scale):
    count = len(blocks)
    each, rows, columns = blocks[0].shape
    size = count * rows
    block = pl.BlockSpec((1, rows, columns), lambda i: (i, 0, 0))
    flops = 2 * each * size * size * (29 * size + 3 * columns)

    def body(*refs):
        orthogonalize_body(scale, count, *refs)

    return pl.pallas_call(
        body,
        grid=(each,),
        in_specs=[block] * count,
        out_specs=[block] * count,
        out_shape=[jax.ShapeDtypeStruct(blocks[0].shape, BF16)] * count,
        scratch_shapes=[
            pltpu.VMEM((size, columns), BF16),
            pltpu.VMEM((size, size), F32),
            pltpu.VMEM((size, size), F32),
        ],
        compiler_params=params(40),
        cost_estimate=cost(flops, 4 * each * size * columns),
        name="orthogonalize",
    )(*blocks)


def grouped(shards):
    groups = []
    top = shards
    for length in (shards // 4,) * 4:
        if length:
            top -= length
            groups.append((top, length))
    return groups if top == 0 else [(0, shards)]


def after(values, *others):
    return lax.optimization_barrier((values, others))[0]


def local(weight, tracker, grad_new, grad_old, mix_keep):
    shards = lax.axis_size("shard")
    _, experts, rows, columns = tracker.shape
    each = experts // shards
    shape = (shards, each, rows, columns)
    weight, tracker, grad_new, grad_old = (
        values.reshape(shape) for values in (weight, tracker, grad_new, grad_old)
    )
    here = lax.axis_index("shard")
    rep_index = lax.axis_index("rep")
    keep = mix_keep.astype(F32) / 16.0
    first, second = keep[rep_index, 0], keep[rep_index, 1]

    def taken(values, start, length):
        return lax.dynamic_slice_in_dim(values, start, length, axis=0)

    new_tracker = jnp.zeros(shape, F32)
    blocks = [None] * shards
    unit = shards // 8
    arrived = []
    ready = None
    for turn, (lowest, length) in enumerate(grouped(shards)):
        if turn == 2:
            tracker = after(tracker, ready)
        start = (here ^ lowest) // length * length
        own = taken(tracker, start, length)
        near = swapped(own.astype(BF16), "rep", 1)
        mixed = first * own + (1.0 - first) * near.astype(F32)
        sent = mixed.astype(BF16)
        if turn == 2:
            sent = after(sent, arrived[1])
        elif turn == 3:
            sent = after(sent, blocks[7 * unit], blocks[6 * unit])
        far = swapped(sent, "rep", 2)
        arrived.append(far)
        if turn == 3:
            far = after(far, blocks[5 * unit], blocks[4 * unit])
        group = second * mixed + (1.0 - second) * far.astype(F32)
        group += taken(grad_new, start, length).astype(F32)
        group -= taken(grad_old, start, length).astype(F32)
        for offset in reversed(range(lowest, lowest + length)):
            block = taken(group, (here ^ offset) % length, 1)[0].astype(BF16)
            if ready is None:
                ready = block
            blocks[offset] = swapped(block, "shard", offset) if offset else block
        new_tracker = lax.dynamic_update_slice_in_dim(new_tracker, group, start, axis=0)

    weight_near = swapped(weight, "rep", 1)
    weight_own = (
        first * weight.astype(F32) + (1.0 - first) * weight_near.astype(F32)
    ).astype(BF16)
    weight_own = after(weight_own, arrived[-1], blocks[1:])
    weight_far = swapped(weight_own, "rep", 2)
    mixed_weight = (
        second * weight_own.astype(F32) + (1.0 - second) * weight_far.astype(F32)
    ).astype(BF16)

    scale = 0.2 * math.sqrt(max(shards * rows, columns))
    updates = orthogonalize(blocks, scale)
    update = jnp.zeros(shape, BF16)
    new_weight = jnp.zeros(shape, BF16)
    half = shards // 2
    order = list(range(1, half)) + list(reversed(range(half, shards))) + [0]
    received = [
        swapped(block, "shard", offset) if offset else block for offset, block in enumerate(updates)
    ]
    mixed_weight = after(mixed_weight, received[-1])
    for offset in order:
        block = received[offset]
        place = here ^ offset
        kept = taken(mixed_weight, place, 1)[0]
        settled = (kept.astype(F32) - learn_rate * block.astype(F32)).astype(BF16)
        update = lax.dynamic_update_slice_in_dim(update, block[None], place, axis=0)
        new_weight = lax.dynamic_update_slice_in_dim(new_weight, settled[None], place, axis=0)
    shape = (1, experts, rows, columns)
    return new_weight.reshape(shape), new_tracker.reshape(shape), update.reshape(shape)


def solution(mesh):
    spec = P("rep", None, "shard", None)
    return jax.shard_map(
        local,
        mesh=mesh,
        in_specs=(spec, spec, spec, spec, P()),
        out_specs=(spec, spec, spec),
        check_vma=False,
    )
```

```python
import math

import jax
import jax.numpy as jnp
from jax import lax
from jax.experimental import pallas as pl
from jax.experimental.pallas import tpu as pltpu
from jax.sharding import PartitionSpec as P

NS_STEPS = 5

coeff_a = 3.4445
coeff_b = -4.775
coeff_c = 2.0315
learn_rate = 0.05

F32 = jnp.float32
BF16 = jnp.bfloat16
MIB = 1 << 20


def swapped(values, axis, offset):
    return lax.ppermute(values, axis, [(i, i ^ offset) for i in range(lax.axis_size(axis))])


def cost(flops, moved):
    return pl.CostEstimate(flops=int(flops), bytes_accessed=int(moved), transcendentals=0)


def params(mib):
    return pltpu.CompilerParams(vmem_limit_bytes=mib * MIB)


def split(values):
    high = values.astype(BF16)
    return high, (values - high.astype(F32)).astype(BF16)


def times(left, right):
    return jnp.dot(left, right, preferred_element_type=F32)


def orthogonalize_body(scale, count, *refs):
    blocks, outs = refs[:count], refs[count : 2 * count]
    held, gram_held, poly_held = refs[2 * count :]
    rows = blocks[0].shape[1]
    for place, block in enumerate(blocks):
        held[pl.ds(place * rows, rows), :] = block[0]
    size = held.shape[0]
    gram = lax.dot_general(
        held[...], held[...], (((1,), (1,)), ((), ())), preferred_element_type=F32
    )
    on_diagonal = lax.broadcasted_iota(jnp.int32, (size, size), 0) == lax.broadcasted_iota(
        jnp.int32, (size, size), 1
    )
    square_norm = jnp.sum(
        jnp.sum(jnp.where(on_diagonal, gram, 0.0), axis=0, keepdims=True), axis=1, keepdims=True
    )
    inverse = 1.0 / (jnp.sqrt(square_norm) + 1e-07)
    gram_held[...] = gram * inverse * inverse

    def step(first, last):
        gram = gram_held[...]
        gram_high, gram_low = split(gram)
        shift = (
            coeff_b * gram_high.astype(F32) + coeff_c * times(gram_high, gram_high)
        ).astype(BF16)
        if first:
            poly_held[...] = jnp.where(on_diagonal, coeff_a, 0.0) + shift.astype(F32)
        else:
            poly = poly_held[...]
            poly_high, poly_low = split(poly)
            poly_held[...] = coeff_a * poly + times(shift, poly_high) + times(shift, poly_low)
        if not last:
            half = coeff_a * gram + times(shift, gram_high) + times(shift, gram_low)
            half_high, half_low = split(half)
            gram_held[...] = coeff_a * half + times(half_high, shift) + times(half_low, shift)

    step(True, False)

    @pl.loop(0, NS_STEPS - 2)
    def _(_):
        step(False, False)

    step(False, True)
    high, low = split(poly_held[...] * (scale * inverse))
    update = (times(high, held[...]) + times(low, held[...])).astype(BF16)
    for place, out in enumerate(outs):
        out[0] = update[place * rows : (place + 1) * rows]


def orthogonalize(blocks, scale):
    count = len(blocks)
    each, rows, columns = blocks[0].shape
    size = count * rows
    block = pl.BlockSpec((1, rows, columns), lambda i: (i, 0, 0))
    flops = 2 * each * size * size * (29 * size + 3 * columns)

    def body(*refs):
        orthogonalize_body(scale, count, *refs)

    return pl.pallas_call(
        body,
        grid=(each,),
        in_specs=[block] * count,
        out_specs=[block] * count,
        out_shape=[jax.ShapeDtypeStruct(blocks[0].shape, BF16)] * count,
        scratch_shapes=[
            pltpu.VMEM((size, columns), BF16),
            pltpu.VMEM((size, size), F32),
            pltpu.VMEM((size, size), F32),
        ],
        compiler_params=params(40),
        cost_estimate=cost(flops, 4 * each * size * columns),
        name="orthogonalize",
    )(*blocks)


def grouped(shards):
    groups = []
    top = shards
    for length in (shards // 8, shards // 8, shards // 4, shards // 2):
        if length:
            top -= length
            groups.append((top, length))
    return groups if top == 0 else [(0, shards)]


def after(values, *others):
    return lax.optimization_barrier((values, others))[0]


def local(weight, tracker, grad_new, grad_old, mix_keep):
    shards = lax.axis_size("shard")
    _, experts, rows, columns = tracker.shape
    each = experts // shards
    shape = (shards, each, rows, columns)
    weight, tracker, grad_new, grad_old = (
        values.reshape(shape) for values in (weight, tracker, grad_new, grad_old)
    )
    here = lax.axis_index("shard")
    rep_index = lax.axis_index("rep")
    keep = mix_keep.astype(F32) / 16.0
    first, second = keep[rep_index, 0], keep[rep_index, 1]

    def taken(values, start, length):
        return lax.dynamic_slice_in_dim(values, start, length, axis=0)

    far_first = keep[rep_index ^ 2, 0]

    def blend(share, own, near):
        return share * own + (1.0 - share) * near.astype(F32)

    new_tracker = jnp.zeros(shape, F32)
    blocks = [None] * shards
    for turn, (lowest, length) in enumerate(grouped(shards)):
        start = (here ^ lowest) // length * length
        own = taken(tracker, start, length)
        rounded = own.astype(BF16)
        mixed = blend(first, own, swapped(rounded, "rep", 1))
        if turn < 2:
            far = swapped(rounded, "rep", 2)
            far_mixed = blend(far_first, far.astype(F32), swapped(far, "rep", 1))
        else:
            far = swapped(mixed.astype(BF16), "rep", 2)
            far_mixed = far.astype(F32)
        group = second * mixed + (1.0 - second) * far_mixed
        group += taken(grad_new, start, length).astype(F32)
        group -= taken(grad_old, start, length).astype(F32)
        for offset in reversed(range(lowest, lowest + length)):
            block = taken(group, (here ^ offset) % length, 1)[0].astype(BF16)
            blocks[offset] = swapped(block, "shard", offset) if offset else block
        new_tracker = lax.dynamic_update_slice_in_dim(new_tracker, group, start, axis=0)

    weight_near = swapped(weight, "rep", 1)
    weight_own = (
        first * weight.astype(F32) + (1.0 - first) * weight_near.astype(F32)
    ).astype(BF16)
    weight_own = after(weight_own, far)
    weight_far = swapped(weight_own, "rep", 2)
    mixed_weight = (
        second * weight_own.astype(F32) + (1.0 - second) * weight_far.astype(F32)
    ).astype(BF16)

    scale = 0.2 * math.sqrt(max(shards * rows, columns))
    updates = orthogonalize(blocks, scale)
    update = jnp.zeros(shape, BF16)
    new_weight = jnp.zeros(shape, BF16)
    half = shards // 2
    order = list(range(1, half)) + list(reversed(range(half, shards))) + [0]
    received = [
        swapped(block, "shard", offset) if offset else block for offset, block in enumerate(updates)
    ]
    mixed_weight = after(mixed_weight, received[-1])
    for offset in order:
        block = received[offset]
        place = here ^ offset
        kept = taken(mixed_weight, place, 1)[0]
        settled = (kept.astype(F32) - learn_rate * block.astype(F32)).astype(BF16)
        update = lax.dynamic_update_slice_in_dim(update, block[None], place, axis=0)
        new_weight = lax.dynamic_update_slice_in_dim(new_weight, settled[None], place, axis=0)
    shape = (1, experts, rows, columns)
    return new_weight.reshape(shape), new_tracker.reshape(shape), update.reshape(shape)


def solution(mesh):
    spec = P("rep", None, "shard", None)
    return jax.shard_map(
        local,
        mesh=mesh,
        in_specs=(spec, spec, spec, spec, P()),
        out_specs=(spec, spec, spec),
        check_vma=False,
    )
```

```python
import math

import jax
import jax.numpy as jnp
from jax import lax
from jax.experimental import pallas as pl
from jax.experimental.pallas import tpu as pltpu
from jax.sharding import PartitionSpec as P

NS_STEPS = 5

coeff_a = 3.4445
coeff_b = -4.775
coeff_c = 2.0315
learn_rate = 0.05

F32 = jnp.float32
BF16 = jnp.bfloat16
MIB = 1 << 20


def swapped(values, axis, offset):
    return lax.ppermute(values, axis, [(i, i ^ offset) for i in range(lax.axis_size(axis))])


def cost(flops, moved):
    return pl.CostEstimate(flops=int(flops), bytes_accessed=int(moved), transcendentals=0)


def params(mib):
    return pltpu.CompilerParams(vmem_limit_bytes=mib * MIB)


def split(values):
    high = values.astype(BF16)
    return high, (values - high.astype(F32)).astype(BF16)


def times(left, right):
    return jnp.dot(left, right, preferred_element_type=F32)


def orthogonalize_body(scale, count, *refs):
    blocks, outs = refs[:count], refs[count : 2 * count]
    held, gram_held, poly_held = refs[2 * count :]
    rows = blocks[0].shape[1]
    for place, block in enumerate(blocks):
        held[pl.ds(place * rows, rows), :] = block[0]
    size = held.shape[0]
    gram = lax.dot_general(
        held[...], held[...], (((1,), (1,)), ((), ())), preferred_element_type=F32
    )
    on_diagonal = lax.broadcasted_iota(jnp.int32, (size, size), 0) == lax.broadcasted_iota(
        jnp.int32, (size, size), 1
    )
    square_norm = jnp.sum(
        jnp.sum(jnp.where(on_diagonal, gram, 0.0), axis=0, keepdims=True), axis=1, keepdims=True
    )
    inverse = 1.0 / (jnp.sqrt(square_norm) + 1e-07)
    gram_held[...] = gram * inverse * inverse

    def step(first, last):
        gram = gram_held[...]
        gram_high, gram_low = split(gram)
        shift = (
            coeff_b * gram_high.astype(F32) + coeff_c * times(gram_high, gram_high)
        ).astype(BF16)
        if first:
            poly_held[...] = jnp.where(on_diagonal, coeff_a, 0.0) + shift.astype(F32)
        else:
            poly = poly_held[...]
            poly_high, poly_low = split(poly)
            poly_held[...] = coeff_a * poly + times(shift, poly_high) + times(shift, poly_low)
        if not last:
            half = coeff_a * gram + times(shift, gram_high) + times(shift, gram_low)
            half_high, half_low = split(half)
            gram_held[...] = coeff_a * half + times(half_high, shift) + times(half_low, shift)

    step(True, False)

    @pl.loop(0, NS_STEPS - 2)
    def _(_):
        step(False, False)

    step(False, True)
    high, low = split(poly_held[...] * (scale * inverse))
    update = (times(high, held[...]) + times(low, held[...])).astype(BF16)
    for place, out in enumerate(outs):
        out[0] = update[place * rows : (place + 1) * rows]


def orthogonalize(blocks, scale):
    count = len(blocks)
    each, rows, columns = blocks[0].shape
    size = count * rows
    block = pl.BlockSpec((1, rows, columns), lambda i: (i, 0, 0))
    flops = 2 * each * size * size * (29 * size + 3 * columns)

    def body(*refs):
        orthogonalize_body(scale, count, *refs)

    return pl.pallas_call(
        body,
        grid=(each,),
        in_specs=[block] * count,
        out_specs=[block] * count,
        out_shape=[jax.ShapeDtypeStruct(blocks[0].shape, BF16)] * count,
        scratch_shapes=[
            pltpu.VMEM((size, columns), BF16),
            pltpu.VMEM((size, size), F32),
            pltpu.VMEM((size, size), F32),
        ],
        compiler_params=params(40),
        cost_estimate=cost(flops, 4 * each * size * columns),
        name="orthogonalize",
    )(*blocks)


def grouped(shards):
    unit = shards // 8
    if shards % 8:
        return [(0, shards)]
    return [(low * unit, count * unit) for low, count in ((7, 1), (6, 1), (2, 2), (4, 2), (0, 2))]


def after(values, *others):
    return lax.optimization_barrier((values, others))[0]


def local(weight, tracker, grad_new, grad_old, mix_keep):
    shards = lax.axis_size("shard")
    _, experts, rows, columns = tracker.shape
    each = experts // shards
    shape = (shards, each, rows, columns)
    weight, tracker, grad_new, grad_old = (
        values.reshape(shape) for values in (weight, tracker, grad_new, grad_old)
    )
    here = lax.axis_index("shard")
    rep_index = lax.axis_index("rep")
    keep = mix_keep.astype(F32) / 16.0
    first, second = keep[rep_index, 0], keep[rep_index, 1]

    def taken(values, start, length):
        return lax.dynamic_slice_in_dim(values, start, length, axis=0)

    far_first = keep[rep_index ^ 2, 0]

    def blend(share, own, near):
        return share * own + (1.0 - share) * near.astype(F32)

    new_tracker = jnp.zeros(shape, F32)
    blocks = [None] * shards
    leads = []
    for turn, (lowest, length) in enumerate(grouped(shards)):
        if turn == 2:
            tracker = after(tracker, leads)
        start = (here ^ lowest) // length * length
        own = taken(tracker, start, length)
        rounded = own.astype(BF16)
        leads.append(rounded)
        mixed = blend(first, own, swapped(rounded, "rep", 1))
        if turn < 2:
            far = swapped(rounded, "rep", 2)
            far_mixed = blend(far_first, far.astype(F32), swapped(far, "rep", 1))
        else:
            far = swapped(mixed.astype(BF16), "rep", 2)
            far_mixed = far.astype(F32)
        base = second * mixed + (
            taken(grad_new, start, length).astype(F32) - taken(grad_old, start, length).astype(F32)
        )
        if turn < 2:
            base = lax.optimization_barrier(base)
        group = base + (1.0 - second) * far_mixed
        for offset in reversed(range(lowest, lowest + length)):
            block = taken(group, (here ^ offset) % length, 1)[0].astype(BF16)
            blocks[offset] = swapped(block, "shard", offset) if offset else block
        new_tracker = lax.dynamic_update_slice_in_dim(new_tracker, group, start, axis=0)

    weight_near = swapped(weight, "rep", 1)
    weight_own = (
        first * weight.astype(F32) + (1.0 - first) * weight_near.astype(F32)
    ).astype(BF16)
    weight_own = after(weight_own, far)
    weight_far = swapped(weight_own, "rep", 2)
    mixed_weight = (
        second * weight_own.astype(F32) + (1.0 - second) * weight_far.astype(F32)
    ).astype(BF16)

    scale = 0.2 * math.sqrt(max(shards * rows, columns))
    updates = orthogonalize(blocks, scale)
    update = jnp.zeros(shape, BF16)
    new_weight = jnp.zeros(shape, BF16)
    half = shards // 2
    order = list(range(1, half)) + list(reversed(range(half, shards))) + [0]
    received = [
        swapped(block, "shard", offset) if offset else block for offset, block in enumerate(updates)
    ]
    mixed_weight = after(mixed_weight, received[-1])
    for offset in order:
        block = received[offset]
        place = here ^ offset
        kept = taken(mixed_weight, place, 1)[0]
        settled = (kept.astype(F32) - learn_rate * block.astype(F32)).astype(BF16)
        update = lax.dynamic_update_slice_in_dim(update, block[None], place, axis=0)
        new_weight = lax.dynamic_update_slice_in_dim(new_weight, settled[None], place, axis=0)
    shape = (1, experts, rows, columns)
    return new_weight.reshape(shape), new_tracker.reshape(shape), update.reshape(shape)


def solution(mesh):
    spec = P("rep", None, "shard", None)
    return jax.shard_map(
        local,
        mesh=mesh,
        in_specs=(spec, spec, spec, spec, P()),
        out_specs=(spec, spec, spec),
        check_vma=False,
    )
```

```python
import math

import jax
import jax.numpy as jnp
from jax import lax
from jax.experimental import pallas as pl
from jax.experimental.pallas import tpu as pltpu
from jax.sharding import PartitionSpec as P

NS_STEPS = 5

coeff_a = 3.4445
coeff_b = -4.775
coeff_c = 2.0315
learn_rate = 0.05

F32 = jnp.float32
BF16 = jnp.bfloat16
MIB = 1 << 20


def swapped(values, axis, offset):
    return lax.ppermute(values, axis, [(i, i ^ offset) for i in range(lax.axis_size(axis))])


def cost(flops, moved):
    return pl.CostEstimate(flops=int(flops), bytes_accessed=int(moved), transcendentals=0)


def params(mib):
    return pltpu.CompilerParams(vmem_limit_bytes=mib * MIB)


def split(values):
    high = values.astype(BF16)
    return high, (values - high.astype(F32)).astype(BF16)


def times(left, right):
    return jnp.dot(left, right, preferred_element_type=F32)


def orthogonalize_body(scale, count, *refs):
    blocks, outs = refs[:count], refs[count : 2 * count]
    held, gram_held, poly_held = refs[2 * count :]
    rows = blocks[0].shape[1]
    for place, block in enumerate(blocks):
        held[pl.ds(place * rows, rows), :] = block[0]
    size = held.shape[0]
    gram = lax.dot_general(
        held[...], held[...], (((1,), (1,)), ((), ())), preferred_element_type=F32
    )
    on_diagonal = lax.broadcasted_iota(jnp.int32, (size, size), 0) == lax.broadcasted_iota(
        jnp.int32, (size, size), 1
    )
    square_norm = jnp.sum(
        jnp.sum(jnp.where(on_diagonal, gram, 0.0), axis=0, keepdims=True), axis=1, keepdims=True
    )
    inverse = 1.0 / (jnp.sqrt(square_norm) + 1e-07)
    gram_held[...] = gram * inverse * inverse

    def step(first, last):
        gram = gram_held[...]
        gram_high, gram_low = split(gram)
        shift = (
            coeff_b * gram_high.astype(F32) + coeff_c * times(gram_high, gram_high)
        ).astype(BF16)
        if first:
            poly_held[...] = jnp.where(on_diagonal, coeff_a, 0.0) + shift.astype(F32)
        else:
            poly = poly_held[...]
            poly_high, poly_low = split(poly)
            poly_held[...] = coeff_a * poly + times(shift, poly_high) + times(shift, poly_low)
        if not last:
            half = coeff_a * gram + times(shift, gram_high) + times(shift, gram_low)
            half_high, half_low = split(half)
            gram_held[...] = coeff_a * half + times(half_high, shift) + times(half_low, shift)

    step(True, False)

    @pl.loop(0, NS_STEPS - 2)
    def _(_):
        step(False, False)

    step(False, True)
    high, low = split(poly_held[...] * (scale * inverse))
    update = (times(high, held[...]) + times(low, held[...])).astype(BF16)
    for place, out in enumerate(outs):
        out[0] = update[place * rows : (place + 1) * rows]


def orthogonalize(blocks, scale):
    count = len(blocks)
    each, rows, columns = blocks[0].shape
    size = count * rows
    block = pl.BlockSpec((1, rows, columns), lambda i: (i, 0, 0))
    flops = 2 * each * size * size * (29 * size + 3 * columns)

    def body(*refs):
        orthogonalize_body(scale, count, *refs)

    return pl.pallas_call(
        body,
        grid=(each,),
        in_specs=[block] * count,
        out_specs=[block] * count,
        out_shape=[jax.ShapeDtypeStruct(blocks[0].shape, BF16)] * count,
        scratch_shapes=[
            pltpu.VMEM((size, columns), BF16),
            pltpu.VMEM((size, size), F32),
            pltpu.VMEM((size, size), F32),
        ],
        compiler_params=params(40),
        cost_estimate=cost(flops, 4 * each * size * columns),
        name="orthogonalize",
    )(*blocks)


def grouped(shards):
    groups = []
    top = shards
    for length in (shards // 8, shards // 8, shards // 4, shards // 2):
        if length:
            top -= length
            groups.append((top, length))
    return groups if top == 0 else [(0, shards)]


def after(values, *others):
    return lax.optimization_barrier((values, others))[0]


def local(weight, tracker, grad_new, grad_old, mix_keep):
    shards = lax.axis_size("shard")
    _, experts, rows, columns = tracker.shape
    each = experts // shards
    shape = (shards, each, rows, columns)
    weight, tracker, grad_new, grad_old = (
        values.reshape(shape) for values in (weight, tracker, grad_new, grad_old)
    )
    here = lax.axis_index("shard")
    rep_index = lax.axis_index("rep")
    keep = mix_keep.astype(F32) / 16.0
    first, second = keep[rep_index, 0], keep[rep_index, 1]

    def taken(values, start, length):
        return lax.dynamic_slice_in_dim(values, start, length, axis=0)

    far_first = keep[rep_index ^ 2, 0]

    def blend(share, own, near):
        return share * own + (1.0 - share) * near.astype(F32)

    new_tracker = jnp.zeros(shape, F32)
    blocks = [None] * shards
    for turn, (lowest, length) in enumerate(grouped(shards)):
        start = (here ^ lowest) // length * length
        own = taken(tracker, start, length)
        rounded = own.astype(BF16)
        mixed = blend(first, own, swapped(rounded, "rep", 1))
        if turn < 2:
            far = swapped(rounded, "rep", 2)
            far_mixed = blend(far_first, far.astype(F32), swapped(far, "rep", 1))
        else:
            far = swapped(mixed.astype(BF16), "rep", 2)
            far_mixed = far.astype(F32)
        base = second * mixed + (
            taken(grad_new, start, length).astype(F32) - taken(grad_old, start, length).astype(F32)
        )
        if turn < 2:
            base = lax.optimization_barrier(base)
        group = base + (1.0 - second) * far_mixed
        offsets = range(lowest, lowest + length)
        for offset in offsets if lowest == 0 else reversed(offsets):
            block = taken(group, (here ^ offset) % length, 1)[0].astype(BF16)
            blocks[offset] = swapped(block, "shard", offset) if offset else block
        new_tracker = lax.dynamic_update_slice_in_dim(new_tracker, group, start, axis=0)

    weight_near = swapped(weight, "rep", 1)
    weight_own = (
        first * weight.astype(F32) + (1.0 - first) * weight_near.astype(F32)
    ).astype(BF16)
    weight_own = after(weight_own, far)
    weight_far = swapped(weight_own, "rep", 2)
    mixed_weight = (
        second * weight_own.astype(F32) + (1.0 - second) * weight_far.astype(F32)
    ).astype(BF16)

    scale = 0.2 * math.sqrt(max(shards * rows, columns))
    updates = orthogonalize(blocks, scale)
    update = jnp.zeros(shape, BF16)
    new_weight = jnp.zeros(shape, BF16)
    half = shards // 2
    order = list(range(1, half)) + list(reversed(range(half, shards))) + [0]
    received = [
        swapped(block, "shard", offset) if offset else block for offset, block in enumerate(updates)
    ]
    mixed_weight = after(mixed_weight, received[-1])
    for offset in order:
        block = received[offset]
        place = here ^ offset
        kept = taken(mixed_weight, place, 1)[0]
        settled = (kept.astype(F32) - learn_rate * block.astype(F32)).astype(BF16)
        update = lax.dynamic_update_slice_in_dim(update, block[None], place, axis=0)
        new_weight = lax.dynamic_update_slice_in_dim(new_weight, settled[None], place, axis=0)
    shape = (1, experts, rows, columns)
    return new_weight.reshape(shape), new_tracker.reshape(shape), update.reshape(shape)


def solution(mesh):
    spec = P("rep", None, "shard", None)
    return jax.shard_map(
        local,
        mesh=mesh,
        in_specs=(spec, spec, spec, spec, P()),
        out_specs=(spec, spec, spec),
        check_vma=False,
    )
```

```python
import math

import jax
import jax.numpy as jnp
from jax import lax
from jax.experimental import pallas as pl
from jax.experimental.pallas import tpu as pltpu
from jax.sharding import PartitionSpec as P

NS_STEPS = 5

coeff_a = 3.4445
coeff_b = -4.775
coeff_c = 2.0315
learn_rate = 0.05

F32 = jnp.float32
BF16 = jnp.bfloat16
MIB = 1 << 20


def swapped(values, axis, offset):
    return lax.ppermute(values, axis, [(i, i ^ offset) for i in range(lax.axis_size(axis))])


def cost(flops, moved):
    return pl.CostEstimate(flops=int(flops), bytes_accessed=int(moved), transcendentals=0)


def params(mib):
    return pltpu.CompilerParams(vmem_limit_bytes=mib * MIB)


def split(values):
    high = values.astype(BF16)
    return high, (values - high.astype(F32)).astype(BF16)


def times(left, right):
    return jnp.dot(left, right, preferred_element_type=F32)


def orthogonalize_body(scale, count, *refs):
    blocks, outs = refs[:count], refs[count : 2 * count]
    held, gram_held, poly_held = refs[2 * count :]
    rows = blocks[0].shape[1]
    for place, block in enumerate(blocks):
        held[pl.ds(place * rows, rows), :] = block[0]
    size = held.shape[0]
    gram = lax.dot_general(
        held[...], held[...], (((1,), (1,)), ((), ())), preferred_element_type=F32
    )
    on_diagonal = lax.broadcasted_iota(jnp.int32, (size, size), 0) == lax.broadcasted_iota(
        jnp.int32, (size, size), 1
    )
    square_norm = jnp.sum(
        jnp.sum(jnp.where(on_diagonal, gram, 0.0), axis=0, keepdims=True), axis=1, keepdims=True
    )
    inverse = 1.0 / (jnp.sqrt(square_norm) + 1e-07)
    gram_held[...] = gram * inverse * inverse

    def step(first, last):
        gram = gram_held[...]
        gram_high, gram_low = split(gram)
        shift = (
            coeff_b * gram_high.astype(F32) + coeff_c * times(gram_high, gram_high)
        ).astype(BF16)
        if first:
            poly_held[...] = jnp.where(on_diagonal, coeff_a, 0.0) + shift.astype(F32)
        else:
            poly = poly_held[...]
            poly_high, poly_low = split(poly)
            poly_held[...] = coeff_a * poly + times(shift, poly_high) + times(shift, poly_low)
        if not last:
            half = coeff_a * gram + times(shift, gram_high) + times(shift, gram_low)
            half_high, half_low = split(half)
            gram_held[...] = coeff_a * half + times(half_high, shift) + times(half_low, shift)

    step(True, False)

    @pl.loop(0, NS_STEPS - 2)
    def _(_):
        step(False, False)

    step(False, True)
    high, low = split(poly_held[...] * (scale * inverse))
    update = (times(high, held[...]) + times(low, held[...])).astype(BF16)
    for place, out in enumerate(outs):
        out[0] = update[place * rows : (place + 1) * rows]


def orthogonalize(blocks, scale):
    count = len(blocks)
    each, rows, columns = blocks[0].shape
    size = count * rows
    block = pl.BlockSpec((1, rows, columns), lambda i: (i, 0, 0))
    flops = 2 * each * size * size * (29 * size + 3 * columns)

    def body(*refs):
        orthogonalize_body(scale, count, *refs)

    return pl.pallas_call(
        body,
        grid=(each,),
        in_specs=[block] * count,
        out_specs=[block] * count,
        out_shape=[jax.ShapeDtypeStruct(blocks[0].shape, BF16)] * count,
        scratch_shapes=[
            pltpu.VMEM((size, columns), BF16),
            pltpu.VMEM((size, size), F32),
            pltpu.VMEM((size, size), F32),
        ],
        compiler_params=params(40),
        cost_estimate=cost(flops, 4 * each * size * columns),
        name="orthogonalize",
    )(*blocks)


def grouped(shards):
    groups = []
    top = shards
    for length in (shards // 8, shards // 8, shards // 4, shards // 2):
        if length:
            top -= length
            groups.append((top, length))
    return groups if top == 0 else [(0, shards)]


def after(values, *others):
    return lax.optimization_barrier((values, others))[0]


def local(weight, tracker, grad_new, grad_old, mix_keep):
    shards = lax.axis_size("shard")
    _, experts, rows, columns = tracker.shape
    each = experts // shards
    shape = (shards, each, rows, columns)
    weight, tracker, grad_new, grad_old = (
        values.reshape(shape) for values in (weight, tracker, grad_new, grad_old)
    )
    here = lax.axis_index("shard")
    rep_index = lax.axis_index("rep")
    keep = mix_keep.astype(F32) / 16.0
    first, second = keep[rep_index, 0], keep[rep_index, 1]

    def taken(values, start, length):
        return lax.dynamic_slice_in_dim(values, start, length, axis=0)

    far_first = keep[rep_index ^ 2, 0]

    def blend(share, own, near):
        return share * own + (1.0 - share) * near.astype(F32)

    new_tracker = jnp.zeros(shape, F32)
    blocks = [None] * shards
    for turn, (lowest, length) in enumerate(grouped(shards)):
        start = (here ^ lowest) // length * length
        own = taken(tracker, start, length)
        rounded = own.astype(BF16)
        mixed = blend(first, own, swapped(rounded, "rep", 1))
        if turn < 2:
            far = swapped(rounded, "rep", 2)
            far_mixed = blend(far_first, far.astype(F32), swapped(far, "rep", 1))
        else:
            far = swapped(mixed.astype(BF16), "rep", 2)
            far_mixed = far.astype(F32)
        base = second * mixed + (
            taken(grad_new, start, length).astype(F32) - taken(grad_old, start, length).astype(F32)
        )
        if turn < 2:
            base = lax.optimization_barrier(base)
        group = base + (1.0 - second) * far_mixed
        offsets = range(lowest, lowest + length)
        for offset in offsets if lowest == 0 else reversed(offsets):
            block = taken(group, (here ^ offset) % length, 1)[0].astype(BF16)
            blocks[offset] = swapped(block, "shard", offset) if offset else block
        new_tracker = lax.dynamic_update_slice_in_dim(new_tracker, group, start, axis=0)

    weight_near = swapped(weight, "rep", 1)
    weight_own = (
        first * weight.astype(F32) + (1.0 - first) * weight_near.astype(F32)
    ).astype(BF16)
    weight_own = after(weight_own, far)
    weight_far = swapped(weight_own, "rep", 2)
    mixed_weight = (
        second * weight_own.astype(F32) + (1.0 - second) * weight_far.astype(F32)
    ).astype(BF16)

    scale = 0.2 * math.sqrt(max(shards * rows, columns))
    half = shards // 2
    rows_order = [0] + list(reversed(range(1, half))) + list(range(half, shards))
    updates = [None] * shards
    for offset, block in zip(rows_order, orthogonalize([blocks[k] for k in rows_order], scale)):
        updates[offset] = block
    update = jnp.zeros(shape, BF16)
    new_weight = jnp.zeros(shape, BF16)
    order = list(range(1, half)) + list(reversed(range(half, shards))) + [0]
    received = [
        swapped(block, "shard", offset) if offset else block for offset, block in enumerate(updates)
    ]
    mixed_weight = after(mixed_weight, received[-1])
    for offset in order:
        block = received[offset]
        place = here ^ offset
        kept = taken(mixed_weight, place, 1)[0]
        settled = (kept.astype(F32) - learn_rate * block.astype(F32)).astype(BF16)
        update = lax.dynamic_update_slice_in_dim(update, block[None], place, axis=0)
        new_weight = lax.dynamic_update_slice_in_dim(new_weight, settled[None], place, axis=0)
    shape = (1, experts, rows, columns)
    return new_weight.reshape(shape), new_tracker.reshape(shape), update.reshape(shape)


def solution(mesh):
    spec = P("rep", None, "shard", None)
    return jax.shard_map(
        local,
        mesh=mesh,
        in_specs=(spec, spec, spec, spec, P()),
        out_specs=(spec, spec, spec),
        check_vma=False,
    )
```

```python
import math

import jax
import jax.numpy as jnp
from jax import lax
from jax.experimental import pallas as pl
from jax.experimental.pallas import tpu as pltpu
from jax.sharding import PartitionSpec as P

NS_STEPS = 5

coeff_a = 3.4445
coeff_b = -4.775
coeff_c = 2.0315
learn_rate = 0.05

F32 = jnp.float32
BF16 = jnp.bfloat16
MIB = 1 << 20


def swapped(values, axis, offset):
    return lax.ppermute(values, axis, [(i, i ^ offset) for i in range(lax.axis_size(axis))])


def cost(flops, moved):
    return pl.CostEstimate(flops=int(flops), bytes_accessed=int(moved), transcendentals=0)


def params(mib):
    return pltpu.CompilerParams(vmem_limit_bytes=mib * MIB)


def split(values):
    high = values.astype(BF16)
    return high, (values - high.astype(F32)).astype(BF16)


def times(left, right):
    return jnp.dot(left, right, preferred_element_type=F32)


def orthogonalize_body(scale, count, *refs):
    blocks, outs = refs[:count], refs[count : 2 * count]
    held, gram_held, poly_held = refs[2 * count :]
    rows = blocks[0].shape[1]
    for place, block in enumerate(blocks):
        held[pl.ds(place * rows, rows), :] = block[0]
    size = held.shape[0]
    gram = lax.dot_general(
        held[...], held[...], (((1,), (1,)), ((), ())), preferred_element_type=F32
    )
    on_diagonal = lax.broadcasted_iota(jnp.int32, (size, size), 0) == lax.broadcasted_iota(
        jnp.int32, (size, size), 1
    )
    square_norm = jnp.sum(
        jnp.sum(jnp.where(on_diagonal, gram, 0.0), axis=0, keepdims=True), axis=1, keepdims=True
    )
    inverse = 1.0 / (jnp.sqrt(square_norm) + 1e-07)
    gram_held[...] = gram * inverse * inverse

    def step(first, last):
        gram = gram_held[...]
        gram_high, gram_low = split(gram)
        shift = (
            coeff_b * gram_high.astype(F32) + coeff_c * times(gram_high, gram_high)
        ).astype(BF16)
        if first:
            poly_held[...] = jnp.where(on_diagonal, coeff_a, 0.0) + shift.astype(F32)
        else:
            poly = poly_held[...]
            poly_high, poly_low = split(poly)
            poly_held[...] = coeff_a * poly + times(shift, poly_high) + times(shift, poly_low)
        if not last:
            half = coeff_a * gram + times(shift, gram_high) + times(shift, gram_low)
            half_high, half_low = split(half)
            gram_held[...] = coeff_a * half + times(half_high, shift) + times(half_low, shift)

    step(True, False)

    @pl.loop(0, NS_STEPS - 2)
    def _(_):
        step(False, False)

    step(False, True)
    high, low = split(poly_held[...] * (scale * inverse))
    update = (times(high, held[...]) + times(low, held[...])).astype(BF16)
    for place, out in enumerate(outs):
        out[0] = update[place * rows : (place + 1) * rows]


def orthogonalize(blocks, scale):
    count = len(blocks)
    each, rows, columns = blocks[0].shape
    size = count * rows
    block = pl.BlockSpec((1, rows, columns), lambda i: (i, 0, 0))
    flops = 2 * each * size * size * (29 * size + 3 * columns)

    def body(*refs):
        orthogonalize_body(scale, count, *refs)

    return pl.pallas_call(
        body,
        grid=(each,),
        in_specs=[block] * count,
        out_specs=[block] * count,
        out_shape=[jax.ShapeDtypeStruct(blocks[0].shape, BF16)] * count,
        scratch_shapes=[
            pltpu.VMEM((size, columns), BF16),
            pltpu.VMEM((size, size), F32),
            pltpu.VMEM((size, size), F32),
        ],
        compiler_params=params(40),
        cost_estimate=cost(flops, 4 * each * size * columns),
        name="orthogonalize",
    )(*blocks)


def grouped(shards):
    unit = shards // 8
    if shards % 8:
        return [[(0, shards)]]
    groups = [[(7, 1)], [(6, 1)], [(2, 2)], [(4, 2)], [(0, 2)]]
    return [[(low * unit, count * unit) for low, count in group] for group in groups]


def after(values, *others):
    return lax.optimization_barrier((values, others))[0]


def local(weight, tracker, grad_new, grad_old, mix_keep):
    shards = lax.axis_size("shard")
    _, experts, rows, columns = tracker.shape
    each = experts // shards
    shape = (shards, each, rows, columns)
    weight, tracker, grad_new, grad_old = (
        values.reshape(shape) for values in (weight, tracker, grad_new, grad_old)
    )
    here = lax.axis_index("shard")
    rep_index = lax.axis_index("rep")
    keep = mix_keep.astype(F32) / 16.0
    first, second = keep[rep_index, 0], keep[rep_index, 1]

    def taken(values, start, length):
        return lax.dynamic_slice_in_dim(values, start, length, axis=0)

    far_first = keep[rep_index ^ 2, 0]

    def blend(share, own, near):
        return share * own + (1.0 - share) * near.astype(F32)

    weight_near = swapped(weight, "rep", 1)
    arrived = []
    new_tracker = jnp.zeros(shape, F32)
    blocks = [None] * shards
    for turn, runs in enumerate(grouped(shards)):
        places = [((here ^ lowest) // length * length, length) for lowest, length in runs]

        def part_of(values):
            parts = [taken(values, start, length) for start, length in places]
            return parts[0] if len(parts) == 1 else jnp.concatenate(parts)

        own = part_of(tracker)
        rounded = own.astype(BF16)
        mixed = blend(first, own, swapped(rounded, "rep", 1))
        if turn < 2:
            far = swapped(rounded, "rep", 2)
            far_mixed = blend(far_first, far.astype(F32), swapped(far, "rep", 1))
        else:
            sent = mixed.astype(BF16)
            if turn == 2:
                sent = after(sent, weight_near)
            elif turn == 4:
                sent = after(sent, arrived[turn - 2], blocks[7 * shards // 8])
            far = swapped(sent, "rep", 2)
            far_mixed = far.astype(F32)
        arrived.append(far)
        base = second * mixed + (part_of(grad_new).astype(F32) - part_of(grad_old).astype(F32))
        if turn < 2:
            base = lax.optimization_barrier(base)
        whole = base + (1.0 - second) * far_mixed
        passed = 0
        for (lowest, length), (start, _) in zip(runs, places):
            group = whole[passed : passed + length]
            passed += length
            for offset in reversed(range(lowest, lowest + length)):
                block = taken(group, (here ^ offset) % length, 1)[0].astype(BF16)
                blocks[offset] = swapped(block, "shard", offset) if offset else block
            new_tracker = lax.dynamic_update_slice_in_dim(new_tracker, group, start, axis=0)

    weight_own = (
        first * weight.astype(F32) + (1.0 - first) * weight_near.astype(F32)
    ).astype(BF16)
    weight_own = after(weight_own, far)
    weight_far = swapped(weight_own, "rep", 2)
    mixed_weight = (
        second * weight_own.astype(F32) + (1.0 - second) * weight_far.astype(F32)
    ).astype(BF16)

    scale = 0.2 * math.sqrt(max(shards * rows, columns))
    updates = orthogonalize(blocks, scale)
    update = jnp.zeros(shape, BF16)
    new_weight = jnp.zeros(shape, BF16)
    half = shards // 2
    order = list(range(1, half)) + list(reversed(range(half, shards))) + [0]
    received = [
        swapped(block, "shard", offset) if offset else block for offset, block in enumerate(updates)
    ]
    mixed_weight = after(mixed_weight, received[-1])
    for offset in order:
        block = received[offset]
        place = here ^ offset
        kept = taken(mixed_weight, place, 1)[0]
        settled = (kept.astype(F32) - learn_rate * block.astype(F32)).astype(BF16)
        update = lax.dynamic_update_slice_in_dim(update, block[None], place, axis=0)
        new_weight = lax.dynamic_update_slice_in_dim(new_weight, settled[None], place, axis=0)
    shape = (1, experts, rows, columns)
    return new_weight.reshape(shape), new_tracker.reshape(shape), update.reshape(shape)


def solution(mesh):
    spec = P("rep", None, "shard", None)
    return jax.shard_map(
        local,
        mesh=mesh,
        in_specs=(spec, spec, spec, spec, P()),
        out_specs=(spec, spec, spec),
        check_vma=False,
    )
```

```python
import math

import jax
import jax.numpy as jnp
from jax import lax
from jax.experimental import pallas as pl
from jax.experimental.pallas import tpu as pltpu
from jax.sharding import PartitionSpec as P

NS_STEPS = 5

coeff_a = 3.4445
coeff_b = -4.775
coeff_c = 2.0315
learn_rate = 0.05

F32 = jnp.float32
BF16 = jnp.bfloat16
MIB = 1 << 20


def swapped(values, axis, offset):
    return lax.ppermute(values, axis, [(i, i ^ offset) for i in range(lax.axis_size(axis))])


def cost(flops, moved):
    return pl.CostEstimate(flops=int(flops), bytes_accessed=int(moved), transcendentals=0)


def params(mib):
    return pltpu.CompilerParams(vmem_limit_bytes=mib * MIB)


def split(values):
    high = values.astype(BF16)
    return high, (values - high.astype(F32)).astype(BF16)


def times(left, right):
    return jnp.dot(left, right, preferred_element_type=F32)


def orthogonalize_body(scale, count, *refs):
    blocks, outs = refs[:count], refs[count : 2 * count]
    held, gram_held, poly_held = refs[2 * count :]
    rows = blocks[0].shape[1]
    for place, block in enumerate(blocks):
        held[pl.ds(place * rows, rows), :] = block[0]
    size = held.shape[0]
    gram = lax.dot_general(
        held[...], held[...], (((1,), (1,)), ((), ())), preferred_element_type=F32
    )
    on_diagonal = lax.broadcasted_iota(jnp.int32, (size, size), 0) == lax.broadcasted_iota(
        jnp.int32, (size, size), 1
    )
    square_norm = jnp.sum(
        jnp.sum(jnp.where(on_diagonal, gram, 0.0), axis=0, keepdims=True), axis=1, keepdims=True
    )
    inverse = 1.0 / (jnp.sqrt(square_norm) + 1e-07)
    gram_held[...] = gram * inverse * inverse

    def step(first, last):
        gram = gram_held[...]
        gram_high, gram_low = split(gram)
        shift = (
            coeff_b * gram_high.astype(F32) + coeff_c * times(gram_high, gram_high)
        ).astype(BF16)
        if first:
            poly_held[...] = jnp.where(on_diagonal, coeff_a, 0.0) + shift.astype(F32)
        else:
            poly = poly_held[...]
            poly_high, poly_low = split(poly)
            poly_held[...] = coeff_a * poly + times(shift, poly_high) + times(shift, poly_low)
        if not last:
            half = coeff_a * gram + times(shift, gram_high) + times(shift, gram_low)
            half_high, half_low = split(half)
            gram_held[...] = coeff_a * half + times(half_high, shift) + times(half_low, shift)

    step(True, False)

    @pl.loop(0, NS_STEPS - 2)
    def _(_):
        step(False, False)

    step(False, True)
    high, low = split(poly_held[...] * (scale * inverse))
    update = (times(high, held[...]) + times(low, held[...])).astype(BF16)
    for place, out in enumerate(outs):
        out[0] = update[place * rows : (place + 1) * rows]


def orthogonalize(blocks, scale):
    count = len(blocks)
    each, rows, columns = blocks[0].shape
    size = count * rows
    block = pl.BlockSpec((1, rows, columns), lambda i: (i, 0, 0))
    flops = 2 * each * size * size * (29 * size + 3 * columns)

    def body(*refs):
        orthogonalize_body(scale, count, *refs)

    return pl.pallas_call(
        body,
        grid=(each,),
        in_specs=[block] * count,
        out_specs=[block] * count,
        out_shape=[jax.ShapeDtypeStruct(blocks[0].shape, BF16)] * count,
        scratch_shapes=[
            pltpu.VMEM((size, columns), BF16),
            pltpu.VMEM((size, size), F32),
            pltpu.VMEM((size, size), F32),
        ],
        compiler_params=params(40),
        cost_estimate=cost(flops, 4 * each * size * columns),
        name="orthogonalize",
    )(*blocks)


def grouped(shards):
    unit = shards // 8
    if shards % 8:
        return [[(0, shards)]]
    groups = [[(7, 1)], [(6, 1)], [(2, 2)], [(4, 2)], [(0, 2)]]
    return [[(low * unit, count * unit) for low, count in group] for group in groups]


def after(values, *others):
    return lax.optimization_barrier((values, others))[0]


def local(weight, tracker, grad_new, grad_old, mix_keep):
    shards = lax.axis_size("shard")
    _, experts, rows, columns = tracker.shape
    each = experts // shards
    shape = (shards, each, rows, columns)
    weight, tracker, grad_new, grad_old = (
        values.reshape(shape) for values in (weight, tracker, grad_new, grad_old)
    )
    here = lax.axis_index("shard")
    rep_index = lax.axis_index("rep")
    keep = mix_keep.astype(F32) / 16.0
    first, second = keep[rep_index, 0], keep[rep_index, 1]

    def taken(values, start, length):
        return lax.dynamic_slice_in_dim(values, start, length, axis=0)

    far_first = keep[rep_index ^ 2, 0]

    def blend(share, own, near):
        return share * own + (1.0 - share) * near.astype(F32)

    weight_near = swapped(weight, "rep", 1)
    arrived = []
    mixes = []
    new_tracker = jnp.zeros(shape, F32)
    blocks = [None] * shards
    for turn, runs in enumerate(grouped(shards)):
        places = [((here ^ lowest) // length * length, length) for lowest, length in runs]

        def part_of(values):
            parts = [taken(values, start, length) for start, length in places]
            return parts[0] if len(parts) == 1 else jnp.concatenate(parts)

        own = part_of(tracker)
        rounded = own.astype(BF16)
        mixed = blend(first, own, swapped(rounded, "rep", 1))
        if turn < 2:
            far = swapped(rounded, "rep", 2)
            far_mixed = blend(far_first, far.astype(F32), swapped(far, "rep", 1))
        else:
            sent = mixed.astype(BF16)
            if turn == 2:
                sent = after(sent, weight_near)
            elif turn == 4:
                sent = after(sent, arrived[2], blocks[7 * shards // 8])
            far = swapped(sent, "rep", 2)
            far_mixed = far.astype(F32)
        arrived.append(far)
        base = second * mixed + (part_of(grad_new).astype(F32) - part_of(grad_old).astype(F32))
        if turn < 2:
            base = lax.optimization_barrier(base)
        whole = base + (1.0 - second) * far_mixed
        passed = 0
        for (lowest, length), (start, _) in zip(runs, places):
            group = whole[passed : passed + length]
            passed += length
            for offset in reversed(range(lowest, lowest + length)):
                block = taken(group, (here ^ offset) % length, 1)[0].astype(BF16)
                blocks[offset] = swapped(block, "shard", offset) if offset else block
            mixes.append((group, start))

    for turn in (0, 1, 3, 2, 4):
        group, start = mixes[turn]
        new_tracker = lax.dynamic_update_slice_in_dim(new_tracker, group, start, axis=0)

    weight_own = (
        first * weight.astype(F32) + (1.0 - first) * weight_near.astype(F32)
    ).astype(BF16)
    weight_own = after(weight_own, far)
    weight_far = swapped(weight_own, "rep", 2)
    mixed_weight = (
        second * weight_own.astype(F32) + (1.0 - second) * weight_far.astype(F32)
    ).astype(BF16)

    scale = 0.2 * math.sqrt(max(shards * rows, columns))
    updates = orthogonalize(blocks, scale)
    update = jnp.zeros(shape, BF16)
    new_weight = jnp.zeros(shape, BF16)
    half = shards // 2
    order = list(range(1, half)) + list(reversed(range(half, shards))) + [0]
    received = [
        swapped(block, "shard", offset) if offset else block for offset, block in enumerate(updates)
    ]
    mixed_weight = after(mixed_weight, received[-1])
    for offset in order:
        block = received[offset]
        place = here ^ offset
        kept = taken(mixed_weight, place, 1)[0]
        settled = (kept.astype(F32) - learn_rate * block.astype(F32)).astype(BF16)
        update = lax.dynamic_update_slice_in_dim(update, block[None], place, axis=0)
        new_weight = lax.dynamic_update_slice_in_dim(new_weight, settled[None], place, axis=0)
    shape = (1, experts, rows, columns)
    return new_weight.reshape(shape), new_tracker.reshape(shape), update.reshape(shape)


def solution(mesh):
    spec = P("rep", None, "shard", None)
    return jax.shard_map(
        local,
        mesh=mesh,
        in_specs=(spec, spec, spec, spec, P()),
        out_specs=(spec, spec, spec),
        check_vma=False,
    )
```

```python
import math

import jax
import jax.numpy as jnp
from jax import lax
from jax.experimental import pallas as pl
from jax.experimental.pallas import tpu as pltpu
from jax.sharding import PartitionSpec as P

NS_STEPS = 5

coeff_a = 3.4445
coeff_b = -4.775
coeff_c = 2.0315
learn_rate = 0.05

F32 = jnp.float32
BF16 = jnp.bfloat16
MIB = 1 << 20


def swapped(values, axis, offset):
    return lax.ppermute(values, axis, [(i, i ^ offset) for i in range(lax.axis_size(axis))])


def cost(flops, moved):
    return pl.CostEstimate(flops=int(flops), bytes_accessed=int(moved), transcendentals=0)


def params(mib):
    return pltpu.CompilerParams(vmem_limit_bytes=mib * MIB)


def split(values):
    high = values.astype(BF16)
    return high, (values - high.astype(F32)).astype(BF16)


def times(left, right):
    return jnp.dot(left, right, preferred_element_type=F32)


def orthogonalize_body(scale, count, *refs):
    blocks, outs = refs[:count], refs[count : 2 * count]
    held, gram_held, poly_held = refs[2 * count :]
    rows = blocks[0].shape[1]
    for place, block in enumerate(blocks):
        held[pl.ds(place * rows, rows), :] = block[0]
    size = held.shape[0]
    gram = lax.dot_general(
        held[...], held[...], (((1,), (1,)), ((), ())), preferred_element_type=F32
    )
    on_diagonal = lax.broadcasted_iota(jnp.int32, (size, size), 0) == lax.broadcasted_iota(
        jnp.int32, (size, size), 1
    )
    square_norm = jnp.sum(
        jnp.sum(jnp.where(on_diagonal, gram, 0.0), axis=0, keepdims=True), axis=1, keepdims=True
    )
    inverse = 1.0 / (jnp.sqrt(square_norm) + 1e-07)
    gram_held[...] = gram * inverse * inverse

    def step(first, last):
        gram = gram_held[...]
        gram_high, gram_low = split(gram)
        shift = (
            coeff_b * gram_high.astype(F32) + coeff_c * times(gram_high, gram_high)
        ).astype(BF16)
        if first:
            poly_held[...] = jnp.where(on_diagonal, coeff_a, 0.0) + shift.astype(F32)
        else:
            poly = poly_held[...]
            poly_high, poly_low = split(poly)
            poly_held[...] = coeff_a * poly + times(shift, poly_high) + times(shift, poly_low)
        if not last:
            half = coeff_a * gram + times(shift, gram_high) + times(shift, gram_low)
            half_high, half_low = split(half)
            gram_held[...] = coeff_a * half + times(half_high, shift) + times(half_low, shift)

    step(True, False)

    @pl.loop(0, NS_STEPS - 2)
    def _(_):
        step(False, False)

    step(False, True)
    high, low = split(poly_held[...] * (scale * inverse))
    update = (times(high, held[...]) + times(low, held[...])).astype(BF16)
    for place, out in enumerate(outs):
        out[0] = update[place * rows : (place + 1) * rows]


def orthogonalize(blocks, scale):
    count = len(blocks)
    each, rows, columns = blocks[0].shape
    size = count * rows
    block = pl.BlockSpec((1, rows, columns), lambda i: (i, 0, 0))
    flops = 2 * each * size * size * (29 * size + 3 * columns)

    def body(*refs):
        orthogonalize_body(scale, count, *refs)

    return pl.pallas_call(
        body,
        grid=(each,),
        in_specs=[block] * count,
        out_specs=[block] * count,
        out_shape=[jax.ShapeDtypeStruct(blocks[0].shape, BF16)] * count,
        scratch_shapes=[
            pltpu.VMEM((size, columns), BF16),
            pltpu.VMEM((size, size), F32),
            pltpu.VMEM((size, size), F32),
        ],
        compiler_params=params(40),
        cost_estimate=cost(flops, 4 * each * size * columns),
        name="orthogonalize",
    )(*blocks)


def grouped(shards):
    unit = shards // 8
    if shards % 8:
        return [[(0, shards)]]
    groups = [[(7, 1)], [(6, 1)], [(2, 2)], [(4, 2)], [(0, 2)]]
    return [[(low * unit, count * unit) for low, count in group] for group in groups]


def after(values, *others):
    return lax.optimization_barrier((values, others))[0]


def local(weight, tracker, grad_new, grad_old, mix_keep):
    shards = lax.axis_size("shard")
    _, experts, rows, columns = tracker.shape
    each = experts // shards
    shape = (shards, each, rows, columns)
    weight, tracker, grad_new, grad_old = (
        values.reshape(shape) for values in (weight, tracker, grad_new, grad_old)
    )
    here = lax.axis_index("shard")
    rep_index = lax.axis_index("rep")
    keep = mix_keep.astype(F32) / 16.0
    first, second = keep[rep_index, 0], keep[rep_index, 1]

    def taken(values, start, length):
        return lax.dynamic_slice_in_dim(values, start, length, axis=0)

    far_first = keep[rep_index ^ 2, 0]

    def blend(share, own, near):
        return share * own + (1.0 - share) * near.astype(F32)

    weight_near = swapped(weight, "rep", 1)
    arrived = []
    mixes = []
    new_tracker = jnp.zeros(shape, F32)
    blocks = [None] * shards
    for turn, runs in enumerate(grouped(shards)):
        places = [((here ^ lowest) // length * length, length) for lowest, length in runs]

        def part_of(values):
            parts = [taken(values, start, length) for start, length in places]
            return parts[0] if len(parts) == 1 else jnp.concatenate(parts)

        own = part_of(tracker)
        rounded = own.astype(BF16)
        mixed = blend(first, own, swapped(rounded, "rep", 1))
        if turn < 2:
            far = swapped(rounded, "rep", 2)
            far_mixed = blend(far_first, far.astype(F32), swapped(far, "rep", 1))
        else:
            sent = mixed.astype(BF16)
            if turn == 2:
                sent = after(sent, weight_near)
            elif turn == 4:
                sent = after(sent, arrived[2], blocks[7 * shards // 8], blocks[6 * shards // 8])
            far = swapped(sent, "rep", 2)
            far_mixed = far.astype(F32)
        arrived.append(far)
        base = second * mixed + (part_of(grad_new).astype(F32) - part_of(grad_old).astype(F32))
        if turn < 2:
            base = lax.optimization_barrier(base)
        whole = base + (1.0 - second) * far_mixed
        passed = 0
        for (lowest, length), (start, _) in zip(runs, places):
            group = whole[passed : passed + length]
            passed += length
            for offset in reversed(range(lowest, lowest + length)):
                block = taken(group, (here ^ offset) % length, 1)[0].astype(BF16)
                blocks[offset] = swapped(block, "shard", offset) if offset else block
            mixes.append((group, start))

    for turn in (0, 1, 3, 2, 4):
        group, start = mixes[turn]
        new_tracker = lax.dynamic_update_slice_in_dim(new_tracker, group, start, axis=0)

    weight_own = (
        first * weight.astype(F32) + (1.0 - first) * weight_near.astype(F32)
    ).astype(BF16)
    weight_own = after(weight_own, far)
    weight_far = swapped(weight_own, "rep", 2)
    mixed_weight = (
        second * weight_own.astype(F32) + (1.0 - second) * weight_far.astype(F32)
    ).astype(BF16)

    scale = 0.2 * math.sqrt(max(shards * rows, columns))
    updates = orthogonalize(blocks, scale)
    update = jnp.zeros(shape, BF16)
    new_weight = jnp.zeros(shape, BF16)
    half = shards // 2
    order = list(range(1, half)) + list(reversed(range(half, shards))) + [0]
    received = [
        swapped(block, "shard", offset) if offset else block for offset, block in enumerate(updates)
    ]
    mixed_weight = after(mixed_weight, received[-1])
    for offset in order:
        block = received[offset]
        place = here ^ offset
        kept = taken(mixed_weight, place, 1)[0]
        settled = (kept.astype(F32) - learn_rate * block.astype(F32)).astype(BF16)
        update = lax.dynamic_update_slice_in_dim(update, block[None], place, axis=0)
        new_weight = lax.dynamic_update_slice_in_dim(new_weight, settled[None], place, axis=0)
    shape = (1, experts, rows, columns)
    return new_weight.reshape(shape), new_tracker.reshape(shape), update.reshape(shape)


def solution(mesh):
    spec = P("rep", None, "shard", None)
    return jax.shard_map(
        local,
        mesh=mesh,
        in_specs=(spec, spec, spec, spec, P()),
        out_specs=(spec, spec, spec),
        check_vma=False,
    )
```

```python
import math

import jax
import jax.numpy as jnp
from jax import lax
from jax.experimental import pallas as pl
from jax.experimental.pallas import tpu as pltpu
from jax.sharding import PartitionSpec as P

NS_STEPS = 5

coeff_a = 3.4445
coeff_b = -4.775
coeff_c = 2.0315
learn_rate = 0.05

F32 = jnp.float32
BF16 = jnp.bfloat16
MIB = 1 << 20


def swapped(values, axis, offset):
    return lax.ppermute(values, axis, [(i, i ^ offset) for i in range(lax.axis_size(axis))])


def cost(flops, moved):
    return pl.CostEstimate(flops=int(flops), bytes_accessed=int(moved), transcendentals=0)


def params(mib):
    return pltpu.CompilerParams(vmem_limit_bytes=mib * MIB)


def split(values):
    high = values.astype(BF16)
    return high, (values - high.astype(F32)).astype(BF16)


def times(left, right):
    return jnp.dot(left, right, preferred_element_type=F32)


def orthogonalize_body(scale, count, *refs):
    blocks, outs = refs[:count], refs[count : 2 * count]
    held, gram_held, poly_held = refs[2 * count :]
    rows = blocks[0].shape[1]
    for place, block in enumerate(blocks):
        held[pl.ds(place * rows, rows), :] = block[0]
    size = held.shape[0]
    gram = lax.dot_general(
        held[...], held[...], (((1,), (1,)), ((), ())), preferred_element_type=F32
    )
    on_diagonal = lax.broadcasted_iota(jnp.int32, (size, size), 0) == lax.broadcasted_iota(
        jnp.int32, (size, size), 1
    )
    square_norm = jnp.sum(
        jnp.sum(jnp.where(on_diagonal, gram, 0.0), axis=0, keepdims=True), axis=1, keepdims=True
    )
    inverse = 1.0 / (jnp.sqrt(square_norm) + 1e-07)
    gram_held[...] = gram * inverse * inverse

    def step(first, last):
        gram = gram_held[...]
        gram_high, gram_low = split(gram)
        shift = (
            coeff_b * gram_high.astype(F32) + coeff_c * times(gram_high, gram_high)
        ).astype(BF16)
        if first:
            poly_held[...] = jnp.where(on_diagonal, coeff_a, 0.0) + shift.astype(F32)
        else:
            poly = poly_held[...]
            poly_high, poly_low = split(poly)
            poly_held[...] = coeff_a * poly + times(shift, poly_high) + times(shift, poly_low)
        if not last:
            half = coeff_a * gram + times(shift, gram_high) + times(shift, gram_low)
            half_high, half_low = split(half)
            gram_held[...] = coeff_a * half + times(half_high, shift) + times(half_low, shift)

    step(True, False)

    @pl.loop(0, NS_STEPS - 2)
    def _(_):
        step(False, False)

    step(False, True)
    high, low = split(poly_held[...] * (scale * inverse))
    update = (times(high, held[...]) + times(low, held[...])).astype(BF16)
    for place, out in enumerate(outs):
        out[0] = update[place * rows : (place + 1) * rows]


def orthogonalize(blocks, scale):
    count = len(blocks)
    each, rows, columns = blocks[0].shape
    size = count * rows
    block = pl.BlockSpec((1, rows, columns), lambda i: (i, 0, 0))
    flops = 2 * each * size * size * (29 * size + 3 * columns)

    def body(*refs):
        orthogonalize_body(scale, count, *refs)

    return pl.pallas_call(
        body,
        grid=(each,),
        in_specs=[block] * count,
        out_specs=[block] * count,
        out_shape=[jax.ShapeDtypeStruct(blocks[0].shape, BF16)] * count,
        scratch_shapes=[
            pltpu.VMEM((size, columns), BF16),
            pltpu.VMEM((size, size), F32),
            pltpu.VMEM((size, size), F32),
        ],
        compiler_params=params(40),
        cost_estimate=cost(flops, 4 * each * size * columns),
        name="orthogonalize",
    )(*blocks)


def grouped(shards):
    unit = shards // 8
    if shards % 8:
        return [[(0, shards)]]
    groups = [[(7, 1)], [(6, 1)], [(2, 2)], [(4, 2)], [(0, 2)]]
    return [[(low * unit, count * unit) for low, count in group] for group in groups]


def after(values, *others):
    return lax.optimization_barrier((values, others))[0]


def local(weight, tracker, grad_new, grad_old, mix_keep):
    shards = lax.axis_size("shard")
    _, experts, rows, columns = tracker.shape
    each = experts // shards
    shape = (shards, each, rows, columns)
    weight, tracker, grad_new, grad_old = (
        values.reshape(shape) for values in (weight, tracker, grad_new, grad_old)
    )
    here = lax.axis_index("shard")
    rep_index = lax.axis_index("rep")
    keep = mix_keep.astype(F32) / 16.0
    first, second = keep[rep_index, 0], keep[rep_index, 1]

    def taken(values, start, length):
        return lax.dynamic_slice_in_dim(values, start, length, axis=0)

    far_first = keep[rep_index ^ 2, 0]

    def blend(share, own, near):
        return share * own + (1.0 - share) * near.astype(F32)

    weight_near = swapped(weight, "rep", 1)
    arrived = []
    mixes = []
    new_tracker = jnp.zeros(shape, F32)
    blocks = [None] * shards
    for turn, runs in enumerate(grouped(shards)):
        places = [((here ^ lowest) // length * length, length) for lowest, length in runs]

        def part_of(values):
            parts = [taken(values, start, length) for start, length in places]
            return parts[0] if len(parts) == 1 else jnp.concatenate(parts)

        own = part_of(tracker)
        rounded = own.astype(BF16)
        mixed = blend(first, own, swapped(rounded, "rep", 1))
        if turn < 2:
            far = swapped(rounded, "rep", 2)
            far_mixed = blend(far_first, far.astype(F32), swapped(far, "rep", 1))
        else:
            sent = mixed.astype(BF16)
            if turn == 2:
                sent = after(sent)
            elif turn == 4:
                sent = after(sent, arrived[2], blocks[7 * shards // 8], weight_near, blocks[6 * shards // 8])
            far = swapped(sent, "rep", 2)
            far_mixed = far.astype(F32)
        arrived.append(far)
        base = second * mixed + (part_of(grad_new).astype(F32) - part_of(grad_old).astype(F32))
        if turn < 2:
            base = lax.optimization_barrier(base)
        whole = base + (1.0 - second) * far_mixed
        passed = 0
        for (lowest, length), (start, _) in zip(runs, places):
            group = whole[passed : passed + length]
            passed += length
            for offset in reversed(range(lowest, lowest + length)):
                block = taken(group, (here ^ offset) % length, 1)[0].astype(BF16)
                blocks[offset] = swapped(block, "shard", offset) if offset else block
            mixes.append((group, start))

    for turn in (0, 1, 3, 2, 4):
        group, start = mixes[turn]
        new_tracker = lax.dynamic_update_slice_in_dim(new_tracker, group, start, axis=0)

    weight_own = (
        first * weight.astype(F32) + (1.0 - first) * weight_near.astype(F32)
    ).astype(BF16)
    weight_own = after(weight_own, far)
    weight_far = swapped(weight_own, "rep", 2)
    mixed_weight = (
        second * weight_own.astype(F32) + (1.0 - second) * weight_far.astype(F32)
    ).astype(BF16)

    scale = 0.2 * math.sqrt(max(shards * rows, columns))
    updates = orthogonalize(blocks, scale)
    update = jnp.zeros(shape, BF16)
    new_weight = jnp.zeros(shape, BF16)
    half = shards // 2
    order = list(range(1, half)) + list(reversed(range(half, shards))) + [0]
    received = [
        swapped(block, "shard", offset) if offset else block for offset, block in enumerate(updates)
    ]
    mixed_weight = after(mixed_weight, received[-1])
    for offset in order:
        block = received[offset]
        place = here ^ offset
        kept = taken(mixed_weight, place, 1)[0]
        settled = (kept.astype(F32) - learn_rate * block.astype(F32)).astype(BF16)
        update = lax.dynamic_update_slice_in_dim(update, block[None], place, axis=0)
        new_weight = lax.dynamic_update_slice_in_dim(new_weight, settled[None], place, axis=0)
    shape = (1, experts, rows, columns)
    return new_weight.reshape(shape), new_tracker.reshape(shape), update.reshape(shape)


def solution(mesh):
    spec = P("rep", None, "shard", None)
    return jax.shard_map(
        local,
        mesh=mesh,
        in_specs=(spec, spec, spec, spec, P()),
        out_specs=(spec, spec, spec),
        check_vma=False,
    )
```

```python
import math

import jax
import jax.numpy as jnp
from jax import lax
from jax.experimental import pallas as pl
from jax.experimental.pallas import tpu as pltpu
from jax.sharding import PartitionSpec as P

NS_STEPS = 5

coeff_a = 3.4445
coeff_b = -4.775
coeff_c = 2.0315
learn_rate = 0.05

F32 = jnp.float32
BF16 = jnp.bfloat16
MIB = 1 << 20


def swapped(values, axis, offset):
    return lax.ppermute(values, axis, [(i, i ^ offset) for i in range(lax.axis_size(axis))])


def cost(flops, moved):
    return pl.CostEstimate(flops=int(flops), bytes_accessed=int(moved), transcendentals=0)


def params(mib):
    return pltpu.CompilerParams(vmem_limit_bytes=mib * MIB)


def split(values):
    high = values.astype(BF16)
    return high, (values - high.astype(F32)).astype(BF16)


def times(left, right):
    return jnp.dot(left, right, preferred_element_type=F32)


def orthogonalize_body(scale, count, *refs):
    blocks, outs = refs[:count], refs[count : 2 * count]
    held, gram_held, poly_held = refs[2 * count :]
    rows = blocks[0].shape[1]
    for place, block in enumerate(blocks):
        held[pl.ds(place * rows, rows), :] = block[0]
    size = held.shape[0]
    gram = lax.dot_general(
        held[...], held[...], (((1,), (1,)), ((), ())), preferred_element_type=F32
    )
    on_diagonal = lax.broadcasted_iota(jnp.int32, (size, size), 0) == lax.broadcasted_iota(
        jnp.int32, (size, size), 1
    )
    square_norm = jnp.sum(
        jnp.sum(jnp.where(on_diagonal, gram, 0.0), axis=0, keepdims=True), axis=1, keepdims=True
    )
    inverse = 1.0 / (jnp.sqrt(square_norm) + 1e-07)
    gram_held[...] = gram * inverse * inverse

    def step(first, last):
        gram = gram_held[...]
        gram_high, gram_low = split(gram)
        shift = (
            coeff_b * gram_high.astype(F32) + coeff_c * times(gram_high, gram_high)
        ).astype(BF16)
        if first:
            poly_held[...] = jnp.where(on_diagonal, coeff_a, 0.0) + shift.astype(F32)
        else:
            poly = poly_held[...]
            poly_high, poly_low = split(poly)
            poly_held[...] = coeff_a * poly + times(shift, poly_high) + times(shift, poly_low)
        if not last:
            half = coeff_a * gram + times(shift, gram_high) + times(shift, gram_low)
            half_high, half_low = split(half)
            gram_held[...] = coeff_a * half + times(half_high, shift) + times(half_low, shift)

    step(True, False)

    @pl.loop(0, NS_STEPS - 2)
    def _(_):
        step(False, False)

    step(False, True)
    high, low = split(poly_held[...] * (scale * inverse))
    update = (times(high, held[...]) + times(low, held[...])).astype(BF16)
    for place, out in enumerate(outs):
        out[0] = update[place * rows : (place + 1) * rows]


def orthogonalize(blocks, scale):
    count = len(blocks)
    each, rows, columns = blocks[0].shape
    size = count * rows
    block = pl.BlockSpec((1, rows, columns), lambda i: (i, 0, 0))
    flops = 2 * each * size * size * (29 * size + 3 * columns)

    def body(*refs):
        orthogonalize_body(scale, count, *refs)

    return pl.pallas_call(
        body,
        grid=(each,),
        in_specs=[block] * count,
        out_specs=[block] * count,
        out_shape=[jax.ShapeDtypeStruct(blocks[0].shape, BF16)] * count,
        scratch_shapes=[
            pltpu.VMEM((size, columns), BF16),
            pltpu.VMEM((size, size), F32),
            pltpu.VMEM((size, size), F32),
        ],
        compiler_params=params(40),
        cost_estimate=cost(flops, 4 * each * size * columns),
        name="orthogonalize",
    )(*blocks)


def grouped(shards):
    unit = shards // 8
    if shards % 8:
        return [[(0, shards)]]
    groups = [[(7, 1)], [(6, 1)], [(2, 2)], [(4, 2)], [(0, 2)]]
    return [[(low * unit, count * unit) for low, count in group] for group in groups]


def after(values, *others):
    return lax.optimization_barrier((values, others))[0]


def local(weight, tracker, grad_new, grad_old, mix_keep):
    shards = lax.axis_size("shard")
    _, experts, rows, columns = tracker.shape
    each = experts // shards
    shape = (shards, each, rows, columns)
    weight, tracker, grad_new, grad_old = (
        values.reshape(shape) for values in (weight, tracker, grad_new, grad_old)
    )
    here = lax.axis_index("shard")
    rep_index = lax.axis_index("rep")
    keep = mix_keep.astype(F32) / 16.0
    first, second = keep[rep_index, 0], keep[rep_index, 1]

    def taken(values, start, length):
        return lax.dynamic_slice_in_dim(values, start, length, axis=0)

    far_first = keep[rep_index ^ 2, 0]

    def blend(share, own, near):
        return share * own + (1.0 - share) * near.astype(F32)

    weight_near = swapped(weight, "rep", 1)
    arrived = []
    mixes = []
    new_tracker = jnp.zeros(shape, F32)
    blocks = [None] * shards
    for turn, runs in enumerate(grouped(shards)):
        places = [((here ^ lowest) // length * length, length) for lowest, length in runs]

        def part_of(values):
            parts = [taken(values, start, length) for start, length in places]
            return parts[0] if len(parts) == 1 else jnp.concatenate(parts)

        own = part_of(tracker)
        rounded = own.astype(BF16)
        mixed = blend(first, own, swapped(rounded, "rep", 1))
        if turn < 2:
            far = swapped(rounded, "rep", 2)
            far_mixed = blend(far_first, far.astype(F32), swapped(far, "rep", 1))
        else:
            sent = mixed.astype(BF16)
            if turn == 2:
                sent = after(sent)
            elif turn == 4:
                sent = after(sent, arrived[2], blocks[7 * shards // 8], weight_near, blocks[6 * shards // 8])
            far = swapped(sent, "rep", 2)
            far_mixed = far.astype(F32)
        arrived.append(far)
        base = second * mixed + (part_of(grad_new).astype(F32) - part_of(grad_old).astype(F32))
        if turn < 2:
            base = lax.optimization_barrier(base)
        whole = base + (1.0 - second) * far_mixed
        passed = 0
        for (lowest, length), (start, _) in zip(runs, places):
            group = whole[passed : passed + length]
            passed += length
            for offset in reversed(range(lowest, lowest + length)):
                block = taken(group, (here ^ offset) % length, 1)[0].astype(BF16)
                blocks[offset] = swapped(block, "shard", offset) if offset else block
            mixes.append((group, start))

    for turn in (0, 1, 3, 2, 4):
        group, start = mixes[turn]
        new_tracker = lax.dynamic_update_slice_in_dim(new_tracker, group, start, axis=0)

    weight_own = (
        first * weight.astype(F32) + (1.0 - first) * weight_near.astype(F32)
    ).astype(BF16)
    weight_own = after(weight_own, far)
    weight_far = swapped(weight_own, "rep", 2)
    mixed_weight = (
        second * weight_own.astype(F32) + (1.0 - second) * weight_far.astype(F32)
    ).astype(BF16)

    scale = 0.2 * math.sqrt(max(shards * rows, columns))
    updates = orthogonalize(blocks, scale)
    update = jnp.zeros(shape, BF16)
    new_weight = jnp.zeros(shape, BF16)
    half = shards // 2
    order = [1, shards - 1, shards - 2, *range(2, half), *reversed(range(half, shards - 2)), 0]
    received = [
        swapped(block, "shard", offset) if offset else block for offset, block in enumerate(updates)
    ]
    mixed_weight = after(mixed_weight, received[-1])
    for offset in order:
        block = received[offset]
        place = here ^ offset
        kept = taken(mixed_weight, place, 1)[0]
        settled = (kept.astype(F32) - learn_rate * block.astype(F32)).astype(BF16)
        update = lax.dynamic_update_slice_in_dim(update, block[None], place, axis=0)
        new_weight = lax.dynamic_update_slice_in_dim(new_weight, settled[None], place, axis=0)
    shape = (1, experts, rows, columns)
    return new_weight.reshape(shape), new_tracker.reshape(shape), update.reshape(shape)


def solution(mesh):
    spec = P("rep", None, "shard", None)
    return jax.shard_map(
        local,
        mesh=mesh,
        in_specs=(spec, spec, spec, spec, P()),
        out_specs=(spec, spec, spec),
        check_vma=False,
    )
```

```python
import math

import jax
import jax.numpy as jnp
from jax import lax
from jax.experimental import pallas as pl
from jax.experimental.pallas import tpu as pltpu
from jax.sharding import PartitionSpec as P

NS_STEPS = 5

coeff_a = 3.4445
coeff_b = -4.775
coeff_c = 2.0315
learn_rate = 0.05

F32 = jnp.float32
BF16 = jnp.bfloat16
MIB = 1 << 20


def swapped(values, axis, offset):
    return lax.ppermute(values, axis, [(i, i ^ offset) for i in range(lax.axis_size(axis))])


def cost(flops, moved):
    return pl.CostEstimate(flops=int(flops), bytes_accessed=int(moved), transcendentals=0)


def params(mib):
    return pltpu.CompilerParams(vmem_limit_bytes=mib * MIB)


def split(values):
    high = values.astype(BF16)
    return high, (values - high.astype(F32)).astype(BF16)


def times(left, right):
    return jnp.dot(left, right, preferred_element_type=F32)


def orthogonalize_body(scale, count, *refs):
    blocks, outs = refs[:count], refs[count : 2 * count]
    held, gram_held, poly_held = refs[2 * count :]
    rows = blocks[0].shape[1]
    for place, block in enumerate(blocks):
        held[pl.ds(place * rows, rows), :] = block[0]
    size = held.shape[0]
    gram = lax.dot_general(
        held[...], held[...], (((1,), (1,)), ((), ())), preferred_element_type=F32
    )
    on_diagonal = lax.broadcasted_iota(jnp.int32, (size, size), 0) == lax.broadcasted_iota(
        jnp.int32, (size, size), 1
    )
    square_norm = jnp.sum(
        jnp.sum(jnp.where(on_diagonal, gram, 0.0), axis=0, keepdims=True), axis=1, keepdims=True
    )
    inverse = 1.0 / (jnp.sqrt(square_norm) + 1e-07)
    gram_held[...] = gram * inverse * inverse

    def step(first, last):
        gram = gram_held[...]
        gram_high, gram_low = split(gram)
        shift = (
            coeff_b * gram_high.astype(F32) + coeff_c * times(gram_high, gram_high)
        ).astype(BF16)
        if first:
            poly_held[...] = jnp.where(on_diagonal, coeff_a, 0.0) + shift.astype(F32)
        else:
            poly = poly_held[...]
            poly_high, poly_low = split(poly)
            poly_held[...] = coeff_a * poly + times(shift, poly_high) + times(shift, poly_low)
        if not last:
            half = coeff_a * gram + times(shift, gram_high) + times(shift, gram_low)
            half_high, half_low = split(half)
            gram_held[...] = coeff_a * half + times(half_high, shift) + times(half_low, shift)

    step(True, False)

    @pl.loop(0, NS_STEPS - 2)
    def _(_):
        step(False, False)

    step(False, True)
    high, low = split(poly_held[...] * (scale * inverse))
    update = (times(high, held[...]) + times(low, held[...])).astype(BF16)
    for place, out in enumerate(outs):
        out[0] = update[place * rows : (place + 1) * rows]


def orthogonalize(blocks, scale):
    count = len(blocks)
    each, rows, columns = blocks[0].shape
    size = count * rows
    block = pl.BlockSpec((1, rows, columns), lambda i: (i, 0, 0))
    flops = 2 * each * size * size * (29 * size + 3 * columns)

    def body(*refs):
        orthogonalize_body(scale, count, *refs)

    return pl.pallas_call(
        body,
        grid=(each,),
        in_specs=[block] * count,
        out_specs=[block] * count,
        out_shape=[jax.ShapeDtypeStruct(blocks[0].shape, BF16)] * count,
        scratch_shapes=[
            pltpu.VMEM((size, columns), BF16),
            pltpu.VMEM((size, size), F32),
            pltpu.VMEM((size, size), F32),
        ],
        compiler_params=params(40),
        cost_estimate=cost(flops, 4 * each * size * columns),
        name="orthogonalize",
    )(*blocks)


def grouped(shards):
    unit = shards // 8
    if shards % 8:
        return [[(0, shards)]]
    groups = [[(7, 1)], [(6, 1)], [(2, 2)], [(4, 2)], [(0, 2)]]
    return [[(low * unit, count * unit) for low, count in group] for group in groups]


def after(values, *others):
    return lax.optimization_barrier((values, others))[0]


def local(weight, tracker, grad_new, grad_old, mix_keep):
    shards = lax.axis_size("shard")
    _, experts, rows, columns = tracker.shape
    each = experts // shards
    shape = (shards, each, rows, columns)
    weight, tracker, grad_new, grad_old = (
        values.reshape(shape) for values in (weight, tracker, grad_new, grad_old)
    )
    here = lax.axis_index("shard")
    rep_index = lax.axis_index("rep")
    keep = mix_keep.astype(F32) / 16.0
    first, second = keep[rep_index, 0], keep[rep_index, 1]

    def taken(values, start, length):
        return lax.dynamic_slice_in_dim(values, start, length, axis=0)

    far_first = keep[rep_index ^ 2, 0]

    def blend(share, own, near):
        return share * own + (1.0 - share) * near.astype(F32)

    weight_near = swapped(weight, "rep", 1)
    weight_own = (
        first * weight.astype(F32) + (1.0 - first) * weight_near.astype(F32)
    ).astype(BF16)
    arrived = []
    mixes = []
    new_tracker = jnp.zeros(shape, F32)
    blocks = [None] * shards
    for turn, runs in enumerate(grouped(shards)):
        places = [((here ^ lowest) // length * length, length) for lowest, length in runs]

        def part_of(values):
            parts = [taken(values, start, length) for start, length in places]
            return parts[0] if len(parts) == 1 else jnp.concatenate(parts)

        own = part_of(tracker)
        rounded = own.astype(BF16)
        mixed = blend(first, own, swapped(rounded, "rep", 1))
        if turn < 2:
            far = swapped(rounded, "rep", 2)
            far_mixed = blend(far_first, far.astype(F32), swapped(far, "rep", 1))
        else:
            sent = mixed.astype(BF16)
            if turn == 2:
                sent = after(sent)
            elif turn == 4:
                sent = after(sent, arrived[2], weight_near)
            far = swapped(sent, "rep", 2)
            if turn == 2:
                far = after(far, weight_own)
            if turn == 4:
                far = after(far, blocks[7 * shards // 8], blocks[6 * shards // 8])
            far_mixed = far.astype(F32)
        arrived.append(far)
        base = second * mixed + (part_of(grad_new).astype(F32) - part_of(grad_old).astype(F32))
        if turn < 2:
            base = lax.optimization_barrier(base)
        whole = base + (1.0 - second) * far_mixed
        passed = 0
        for (lowest, length), (start, _) in zip(runs, places):
            group = whole[passed : passed + length]
            passed += length
            for offset in reversed(range(lowest, lowest + length)):
                block = taken(group, (here ^ offset) % length, 1)[0].astype(BF16)
                blocks[offset] = swapped(block, "shard", offset) if offset else block
            mixes.append((group, start))

    for turn in (0, 1, 3, 2, 4):
        group, start = mixes[turn]
        new_tracker = lax.dynamic_update_slice_in_dim(new_tracker, group, start, axis=0)

    weight_own = after(weight_own, far)
    weight_far = swapped(weight_own, "rep", 2)
    mixed_weight = (
        second * weight_own.astype(F32) + (1.0 - second) * weight_far.astype(F32)
    ).astype(BF16)

    scale = 0.2 * math.sqrt(max(shards * rows, columns))
    updates = orthogonalize(blocks, scale)
    update = jnp.zeros(shape, BF16)
    new_weight = jnp.zeros(shape, BF16)
    half = shards // 2
    order = [1, shards - 1, shards - 2, *range(2, half), *reversed(range(half, shards - 2)), 0]
    received = [
        swapped(block, "shard", offset) if offset else block for offset, block in enumerate(updates)
    ]
    mixed_weight = after(mixed_weight, received[-1])
    for offset in order:
        block = received[offset]
        place = here ^ offset
        kept = taken(mixed_weight, place, 1)[0]
        settled = (kept.astype(F32) - learn_rate * block.astype(F32)).astype(BF16)
        update = lax.dynamic_update_slice_in_dim(update, block[None], place, axis=0)
        new_weight = lax.dynamic_update_slice_in_dim(new_weight, settled[None], place, axis=0)
    shape = (1, experts, rows, columns)
    return new_weight.reshape(shape), new_tracker.reshape(shape), update.reshape(shape)


def solution(mesh):
    spec = P("rep", None, "shard", None)
    return jax.shard_map(
        local,
        mesh=mesh,
        in_specs=(spec, spec, spec, spec, P()),
        out_specs=(spec, spec, spec),
        check_vma=False,
    )
```

```python
import math

import jax
import jax.numpy as jnp
from jax import lax
from jax.experimental import pallas as pl
from jax.experimental.pallas import tpu as pltpu
from jax.sharding import PartitionSpec as P

NS_STEPS = 5

coeff_a = 3.4445
coeff_b = -4.775
coeff_c = 2.0315
learn_rate = 0.05

F32 = jnp.float32
BF16 = jnp.bfloat16
MIB = 1 << 20


def swapped(values, axis, offset):
    return lax.ppermute(values, axis, [(i, i ^ offset) for i in range(lax.axis_size(axis))])


def cost(flops, moved):
    return pl.CostEstimate(flops=int(flops), bytes_accessed=int(moved), transcendentals=0)


def params(mib):
    return pltpu.CompilerParams(vmem_limit_bytes=mib * MIB)


def split(values):
    high = values.astype(BF16)
    return high, (values - high.astype(F32)).astype(BF16)


def times(left, right):
    return jnp.dot(left, right, preferred_element_type=F32)


def orthogonalize_body(scale, count, *refs):
    blocks, outs = refs[:count], refs[count : 2 * count]
    held, gram_held, poly_held = refs[2 * count :]
    rows = blocks[0].shape[1]
    for place, block in enumerate(blocks):
        held[pl.ds(place * rows, rows), :] = block[0]
    size = held.shape[0]
    gram = lax.dot_general(
        held[...], held[...], (((1,), (1,)), ((), ())), preferred_element_type=F32
    )
    on_diagonal = lax.broadcasted_iota(jnp.int32, (size, size), 0) == lax.broadcasted_iota(
        jnp.int32, (size, size), 1
    )
    square_norm = jnp.sum(
        jnp.sum(jnp.where(on_diagonal, gram, 0.0), axis=0, keepdims=True), axis=1, keepdims=True
    )
    inverse = 1.0 / (jnp.sqrt(square_norm) + 1e-07)
    gram_held[...] = gram * inverse * inverse

    def step(first, last):
        gram = gram_held[...]
        gram_high, gram_low = split(gram)
        shift = (
            coeff_b * gram_high.astype(F32) + coeff_c * times(gram_high, gram_high)
        ).astype(BF16)
        if first:
            poly_held[...] = jnp.where(on_diagonal, coeff_a, 0.0) + shift.astype(F32)
        else:
            poly = poly_held[...]
            poly_high, poly_low = split(poly)
            poly_held[...] = coeff_a * poly + times(shift, poly_high) + times(shift, poly_low)
        if not last:
            half = coeff_a * gram + times(shift, gram_high) + times(shift, gram_low)
            half_high, half_low = split(half)
            gram_held[...] = coeff_a * half + times(half_high, shift) + times(half_low, shift)

    step(True, False)

    @pl.loop(0, NS_STEPS - 2)
    def _(_):
        step(False, False)

    step(False, True)
    high, low = split(poly_held[...] * (scale * inverse))
    update = (times(high, held[...]) + times(low, held[...])).astype(BF16)
    for place, out in enumerate(outs):
        out[0] = update[place * rows : (place + 1) * rows]


def orthogonalize(blocks, scale):
    count = len(blocks)
    each, rows, columns = blocks[0].shape
    size = count * rows
    block = pl.BlockSpec((1, rows, columns), lambda i: (i, 0, 0))
    flops = 2 * each * size * size * (29 * size + 3 * columns)

    def body(*refs):
        orthogonalize_body(scale, count, *refs)

    return pl.pallas_call(
        body,
        grid=(each,),
        in_specs=[block] * count,
        out_specs=[block] * count,
        out_shape=[jax.ShapeDtypeStruct(blocks[0].shape, BF16)] * count,
        scratch_shapes=[
            pltpu.VMEM((size, columns), BF16),
            pltpu.VMEM((size, size), F32),
            pltpu.VMEM((size, size), F32),
        ],
        compiler_params=params(40),
        cost_estimate=cost(flops, 4 * each * size * columns),
        name="orthogonalize",
    )(*blocks)


def grouped(shards):
    unit = shards // 8
    if shards % 8:
        return [[(0, shards)]]
    groups = [[(7, 1)], [(6, 1)], [(2, 2)], [(4, 2)], [(0, 2)]]
    return [[(low * unit, count * unit) for low, count in group] for group in groups]


def after(values, *others):
    return lax.optimization_barrier((values, others))[0]


def local(weight, tracker, grad_new, grad_old, mix_keep):
    shards = lax.axis_size("shard")
    _, experts, rows, columns = tracker.shape
    each = experts // shards
    shape = (shards, each, rows, columns)
    weight, tracker, grad_new, grad_old = (
        values.reshape(shape) for values in (weight, tracker, grad_new, grad_old)
    )
    here = lax.axis_index("shard")
    rep_index = lax.axis_index("rep")
    keep = mix_keep.astype(F32) / 16.0
    first, second = keep[rep_index, 0], keep[rep_index, 1]

    def taken(values, start, length):
        return lax.dynamic_slice_in_dim(values, start, length, axis=0)

    far_first = keep[rep_index ^ 2, 0]

    def blend(share, own, near):
        return share * own + (1.0 - share) * near.astype(F32)

    weight_near = swapped(weight, "rep", 1)
    weight_own = (
        first * weight.astype(F32) + (1.0 - first) * weight_near.astype(F32)
    ).astype(BF16)
    arrived = []
    mixes = []
    new_tracker = jnp.zeros(shape, F32)
    blocks = [None] * shards
    for turn, runs in enumerate(grouped(shards)):
        places = [((here ^ lowest) // length * length, length) for lowest, length in runs]

        def part_of(values):
            parts = [taken(values, start, length) for start, length in places]
            return parts[0] if len(parts) == 1 else jnp.concatenate(parts)

        own = part_of(tracker)
        rounded = own.astype(BF16)
        mixed = blend(first, own, swapped(rounded, "rep", 1))
        if turn < 2:
            far = swapped(rounded, "rep", 2)
            far_mixed = blend(far_first, far.astype(F32), swapped(far, "rep", 1))
        else:
            sent = mixed.astype(BF16)
            if turn == 2:
                sent = after(sent)
            elif turn == 4:
                sent = after(sent, arrived[2], weight_near)
            far = swapped(sent, "rep", 2)
            if turn == 3:
                far = after(far, weight_own)
            if turn == 4:
                far = after(far, blocks[7 * shards // 8], blocks[6 * shards // 8])
            far_mixed = far.astype(F32)
        arrived.append(far)
        base = second * mixed + (part_of(grad_new).astype(F32) - part_of(grad_old).astype(F32))
        if turn < 2:
            base = lax.optimization_barrier(base)
        whole = base + (1.0 - second) * far_mixed
        passed = 0
        for (lowest, length), (start, _) in zip(runs, places):
            group = whole[passed : passed + length]
            passed += length
            for offset in reversed(range(lowest, lowest + length)):
                block = taken(group, (here ^ offset) % length, 1)[0].astype(BF16)
                blocks[offset] = swapped(block, "shard", offset) if offset else block
            mixes.append((group, start))

    for turn in (0, 1, 3, 2, 4):
        group, start = mixes[turn]
        new_tracker = lax.dynamic_update_slice_in_dim(new_tracker, group, start, axis=0)

    weight_own = after(weight_own, far)
    weight_far = swapped(weight_own, "rep", 2)
    mixed_weight = (
        second * weight_own.astype(F32) + (1.0 - second) * weight_far.astype(F32)
    ).astype(BF16)

    scale = 0.2 * math.sqrt(max(shards * rows, columns))
    updates = orthogonalize(blocks, scale)
    update = jnp.zeros(shape, BF16)
    new_weight = jnp.zeros(shape, BF16)
    half = shards // 2
    order = [1, shards - 1, shards - 2, *range(2, half), *reversed(range(half, shards - 2)), 0]
    received = [
        swapped(block, "shard", offset) if offset else block for offset, block in enumerate(updates)
    ]
    mixed_weight = after(mixed_weight, received[-1])
    for offset in order:
        block = received[offset]
        place = here ^ offset
        kept = taken(mixed_weight, place, 1)[0]
        settled = (kept.astype(F32) - learn_rate * block.astype(F32)).astype(BF16)
        update = lax.dynamic_update_slice_in_dim(update, block[None], place, axis=0)
        new_weight = lax.dynamic_update_slice_in_dim(new_weight, settled[None], place, axis=0)
    shape = (1, experts, rows, columns)
    return new_weight.reshape(shape), new_tracker.reshape(shape), update.reshape(shape)


def solution(mesh):
    spec = P("rep", None, "shard", None)
    return jax.shard_map(
        local,
        mesh=mesh,
        in_specs=(spec, spec, spec, spec, P()),
        out_specs=(spec, spec, spec),
        check_vma=False,
    )
```
